128 devices in a mesh: dp: 64 (over x_hi, y, z, core), sub: 2 (over x_lo).
Axes of the slice: x: 4 (x_hi: 2, x_lo: 2; x = x_hi * 2 + x_lo), y: 4, z: 4, core: 2. Of those that a mesh axis runs over, the one named last changes fastest.
Arguments:
- images: bfloat16 [65536, 1152], P(('dp', 'sub')), may hold values from -1 to 1
- text_embeds: bfloat16 [65536, 1152], P('dp'), may hold values from -3 to 3
- dest_slot: int32 [65536], P(('dp', 'sub')), may hold values from -1 to 32767, as said below
- labels: int32 [32768], P(('dp', 'sub')), may hold values from 0 to 65535, as said below
- logit_scale: float32 [1], replicated, may hold values from 2 to 6
- logit_bias: float32 [1], replicated, may hold values from -3 to -1
Outputs:
- grad_images: bfloat16 [65536, 1152], P(('dp', 'sub'))
- grad_text: float32 [65536, 1152], P(('dp', 'sub'))
- loss: float32 [1], replicated
- grad_scale: float32 [1], replicated
- grad_bias: float32 [1], replicated
The draws below stay inside these ranges and needn't reach their ends.
Inputs may be any that keep to these rules, and one draw needn't show every extreme that they name: `dest_slot`: every slot is named by exactly one packed row. At most 4 packed rows of one device name slots of one device, and every device receives exactly 4 rows from half of the devices; one device has no padding rows. labels[i] names a text whose block is (i // 512 - s) mod 64 for some s in 0 .. 3.
All inputs are finite; a program needn't handle non-finite values.
Results may differ from the reference program's by a relative error of at most 0.0034.
Values may be sent and summed in bfloat16 or wider, within the bound.
A program may use at most 128 MiB of HBM per device.

```python
import jax
import jax.numpy as jnp
from jax import lax

D = 1152
C = 4
TXT_DP = 1024
STOPS = 4
IMG_DEV = 256
PACKED = 65536
GROUP = 512
TEXTS = 65536
N_DP = 64
N_SUB = 2


def entry_draw(key, rows, spread):
    first_key = jax.random.fold_in(key, 0)
    base = jax.random.truncated_normal(first_key, -4.0, 4.0, (rows, D), jnp.float32)
    return base * spread


def draw_images(key, part):
    key = jax.random.fold_in(key, 13)
    return entry_draw(key, PACKED, 0.12).astype(jnp.bfloat16)


def draw_text_embeds(key, part):
    key = jax.random.fold_in(key, 14)
    block = (jnp.arange(TEXTS) // TXT_DP).astype(jnp.float32)
    ramp = 0.5 + 2.0 * block / max(N_DP - 1, 1)
    return (entry_draw(key, TEXTS, 0.12) * ramp[:, None]).astype(jnp.bfloat16)


def draw_dest_slot(key, part):
    key = jax.random.fold_in(key, 11)
    devices = N_DP * N_SUB
    capacity = C * devices
    first_key, second_key, third_key, fourth_key = jax.random.split(key, 4)
    special = jax.random.randint(first_key, (), 0, devices)
    ranking = jax.vmap(lambda each_key: jax.random.permutation(each_key, devices))(jax.random.split(second_key, devices))
    special_rank = ranking[:, special][:, None]
    sources = jnp.arange(devices)[None, :]
    ranking = jnp.where(sources == special, 0, jnp.where(ranking < special_rank, ranking + 1, ranking))
    sent_rows = jnp.where(ranking < devices // 2, C, 0).T
    start_src = jnp.cumsum(sent_rows, axis=1) - sent_rows
    start_dst = jnp.cumsum(sent_rows, axis=0) - sent_rows
    slot_order = jax.vmap(lambda each_key: jax.random.permutation(each_key, IMG_DEV))(jax.random.split(third_key, devices))
    shuffles = jax.vmap(lambda each_key: jax.random.permutation(each_key, capacity))(jax.random.split(fourth_key, devices))
    within = jnp.arange(C)[None, None, :]
    live_rows = within < sent_rows[:, :, None]
    packed_pos = jnp.minimum(start_src[:, :, None] + within, capacity - 1)
    local_slot = jnp.minimum(start_dst[:, :, None] + within, IMG_DEV - 1)
    dest_index = jnp.arange(devices)[None, :, None]
    global_slot = dest_index * IMG_DEV + slot_order[dest_index, local_slot]
    source_index = jnp.arange(devices)[:, None, None]
    final_row = source_index * capacity + shuffles[source_index, packed_pos]
    row_index = jnp.where(live_rows, final_row, devices * capacity)
    result = jnp.full((devices * capacity,), -1, jnp.int32)
    result = result.at[row_index.reshape(-1)].set(global_slot.reshape(-1).astype(jnp.int32), mode='drop')
    return result.astype(jnp.int32)


def draw_labels(key, part):
    key = jax.random.fold_in(key, 12)
    first_key, second_key = jax.random.split(key, 2)
    total = IMG_DEV * N_DP * N_SUB
    group_index = jnp.arange(total) // (IMG_DEV * N_SUB)
    steps_back = jax.random.randint(first_key, (total,), 0, STOPS)
    chosen = jax.random.randint(second_key, (total,), 0, TXT_DP)
    return ((group_index - steps_back) % N_DP * TXT_DP + chosen).astype(jnp.int32)


def setup_inputs(seed: int = 0) -> dict:
    key_list = jax.random.split(jax.random.key(seed), 7)
    return {
        "images": draw_images(jax.random.fold_in(key_list[6], 71), 0),
        "text_embeds": draw_text_embeds(jax.random.fold_in(key_list[6], 71), 0),
        "dest_slot": draw_dest_slot(jax.random.fold_in(key_list[6], 71), 0),
        "labels": draw_labels(jax.random.fold_in(key_list[6], 71), 0),
        "logit_scale": jnp.clip(jax.random.uniform(key_list[4], (1,), jnp.float32, 2.0, 6.0), 2.0, 6.0),
        "logit_bias": jnp.clip(jax.random.uniform(key_list[5], (1,), jnp.float32, -3.0, -1.0), -3.0, -1.0),
    }


def group_terms(operands):
    slot_rows, block_rows, group_labels, owner_block, factor, offset = operands
    inner = jnp.dot(slot_rows, block_rows.T, preferred_element_type=jnp.float32)
    logits = factor * inner + offset
    text_ids = owner_block * TXT_DP + jnp.arange(TXT_DP).astype(jnp.int32)
    positive = group_labels[:, None] == text_ids[None, :]
    label_sign = jnp.where(positive, 1.0, -1.0).astype(jnp.float32)
    loss_sum = -jnp.sum(jax.nn.log_sigmoid(label_sign * logits))
    logit_grad = jax.nn.sigmoid(logits) - positive.astype(jnp.float32)
    scale_sum = jnp.sum(logit_grad * inner)
    bias_sum = jnp.sum(logit_grad)
    weights = logit_grad.astype(jnp.bfloat16)
    image_term = jnp.dot(weights, block_rows, preferred_element_type=jnp.float32)
    text_term = jnp.dot(weights.T, slot_rows, preferred_element_type=jnp.float32)
    return image_term, text_term, jnp.stack([loss_sum, scale_sum, bias_sum])


def reference(images, text_embeds, dest_slot, labels, logit_scale, logit_bias):
    devices = N_DP * N_SUB
    slots = IMG_DEV * devices
    occupied = dest_slot >= 0
    target = jnp.where(occupied, dest_slot, slots).astype(jnp.int32)
    slotted = jnp.zeros((slots, D), jnp.bfloat16).at[target].set(images, mode="drop")
    groups = slotted.reshape(N_DP, GROUP, D)
    group_labels = labels.reshape(N_DP, GROUP)
    blocks = text_embeds.reshape(N_DP, TXT_DP, D)
    factor = logit_scale[0]
    offset = logit_bias[0]
    image_sum = jnp.zeros((N_DP, GROUP, D), jnp.float32)
    text_sum = jnp.zeros((N_DP, TXT_DP, D), jnp.float32)
    totals = jnp.zeros((3,), jnp.float32)
    for visit in range(STOPS):
        visiting = jnp.roll(blocks, visit, axis=0)
        owners = ((jnp.arange(N_DP) - visit) % N_DP).astype(jnp.int32)
        factors = jnp.full((N_DP,), factor, jnp.float32)
        offsets = jnp.full((N_DP,), offset, jnp.float32)
        image_term, text_term, stats_now = lax.map(group_terms, (groups, visiting, group_labels, owners, factors, offsets))
        image_sum = image_sum + image_term
        text_sum = text_sum + jnp.roll(text_term, -visit, axis=0)
        totals = totals + jnp.sum(stats_now, axis=0)
    slot_grad = (factor * image_sum).astype(jnp.bfloat16).reshape(slots, D)
    picked = jnp.take(slot_grad, jnp.minimum(target, slots - 1), axis=0)
    grad_images = jnp.where(occupied[:, None], picked, jnp.zeros_like(picked))
    grad_text = (factor * text_sum).reshape(TEXTS, D)
    pair_count = float(slots * STOPS * TXT_DP)
    loss = (totals[0] / pair_count).reshape(1)
    grad_scale = (totals[1] / pair_count).reshape(1)
    grad_bias = (totals[2] / pair_count).reshape(1)
    return grad_images, grad_text, loss, grad_scale, grad_bias
```

```python
import functools

import jax
import jax.numpy as jnp
from jax import lax
from jax.experimental import pallas as pl
from jax.experimental.pallas import tpu as pltpu
from jax.sharding import PartitionSpec as P

STOPS = 4
LANES = 128
MESH = pl.DeviceIdType.MESH
F32 = jnp.float32
BF16 = jnp.bfloat16


def iota(shape, axis):
    return lax.broadcasted_iota(jnp.int32, shape, axis)


def mm(a, b):
    return lax.dot_general(a, b, (((1,), (0,)), ((), ())), preferred_element_type=F32)


def mm_nt(a, b):
    return lax.dot_general(a, b, (((1,), (1,)), ((), ())), preferred_element_type=F32)


def kernel(
    n_dp,
    pairs,
    scale_ref,
    bias_ref,
    dest_ref,
    labels_ref,
    images_ref,
    text_ref,
    gi_ref,
    gt_ref,
    loss_ref,
    gscale_ref,
    gbias_ref,
    send,
    recv,
    back,
    back_recv,
    home,
    part,
    part_in,
    sl,
    lab,
    wt,
    wn,
    own,
    own_in,
    pre,
    pre_in,
    ret1_out,
    ret1,
    ret2_out,
    ret2,
    ret2b,
    slot_grad,
    text_out,
    text_in,
    p_t,
    q_t,
    stat,
    stat_in,
    a2a_send,
    a2a_recv,
    local_sem,
    ss,
    rs,
):
    rows, columns = images_ref.shape
    texts = text_ref.shape[0]
    slots = labels_ref.shape[1]
    half = slots // 2
    chips = n_dp
    n_m = n_dp // 2
    per_chip = rows // chips
    width = send.shape[2]
    tail = columns - width
    t_tile = min(256, texts // 2)

    d = lax.axis_index("dp")
    s = lax.axis_index("sub")
    m = lax.div(d, 2)
    c = lax.rem(d, 2)
    chip = m * 2 + s
    partner = (m * 2 + (1 - c), s)
    across = (d, 1 - s)

    def chip_dev(i):
        i = lax.rem(i + chips, chips)
        return (lax.div(i, 2) * 2 + c, lax.rem(i, 2))

    def m_dev(step):
        return (lax.rem(m + step + n_m, n_m) * 2 + c, s)

    def dp_dev(step):
        return (lax.rem(d + step + n_dp, n_dp), s)

    barrier = pltpu.get_barrier_semaphore()

    def greet(k, carry):
        pl.semaphore_signal(barrier, inc=1, device_id=chip_dev(chip + k), device_id_type=MESH)
        return carry

    lax.fori_loop(1, chips, greet, 0)
    for dev in (partner, dp_dev(1), dp_dev(3)):
        pl.semaphore_signal(barrier, inc=1, device_id=dev, device_id_type=MESH)

    def remote(src, dst, k, dev):
        return pltpu.make_async_remote_copy(
            src_ref=src,
            dst_ref=dst,
            send_sem=ss.at[k],
            recv_sem=rs.at[k],
            device_id=dev,
            device_id_type=MESH,
        )

    q = dest_ref[...]
    valid = q >= 0
    group = lax.div(jnp.maximum(q, 0), 2 * slots)
    rest = jnp.maximum(q, 0) - group * (2 * slots)
    to_sub = lax.div(rest, slots)
    slot_id = rest - to_sub * slots
    even = (group & 1) == 0
    to_m = lax.div((group + (n_dp - 1)) & (n_dp - 1), 2)
    rel = (to_m * 2 + to_sub - chip + (chips - 1)) & (chips - 1)
    rel = jnp.where(valid, rel, -1)
    onehot = rel == iota((chips, rows), 0)
    earlier = (iota((rows, rows), 0) < iota((rows, rows), 1)).astype(F32).astype(BF16)
    onehot_f = onehot.astype(F32)
    rank = mm(onehot_f.astype(BF16), earlier)
    within = jnp.sum(onehot_f * rank, axis=0, keepdims=True)
    placed = jnp.where(valid, rel.astype(F32) * float(per_chip) + within, -1.0)
    placed_col = jnp.transpose(jnp.broadcast_to(placed, (LANES, rows)))[:, :1].astype(jnp.int32)
    p_t[...] = (placed_col == iota((rows, rows), 1)).astype(F32).astype(BF16)
    placed_int = placed.astype(jnp.int32)
    id_plus = (slot_id + 1).astype(F32)
    id_odd = jnp.where(valid & jnp.logical_not(even), id_plus, 0.0)
    id_even = jnp.where(valid & even, id_plus, 0.0)
    which = iota((LANES, rows), 0)
    id_rows = jnp.where(which == 0, id_odd, jnp.where(which == 1, id_even, 0.0))
    ids_block = jnp.transpose(id_rows).astype(BF16)
    row_tile = min(128, rows)
    for r in range(rows // row_tile):
        p_mat = (placed_int == iota((row_tile, rows), 0) + r * row_tile).astype(F32).astype(BF16)
        n = row_tile // per_chip
        first = mm(p_mat, images_ref[:, :width]).reshape(n, per_chip, width)
        second = mm(p_mat, images_ref[:, width:]).reshape(n, per_chip, tail)
        third = mm(p_mat, ids_block).reshape(n, per_chip, LANES)
        second = jnp.concatenate([second, third], axis=2)
        send[r * n : (r + 1) * n] = jnp.concatenate([first, second], axis=1).astype(BF16)

    pl.semaphore_wait(barrier, chips - 1 + 3)

    lab_copies = [
        remote(labels_ref, lab.at[slot], 9 + step, dp_dev(-step))
        for step, slot in ((1, 1 - c), (2, 1 + c), (3, 3 - c))
    ]
    for copy in lab_copies:
        copy.start()
    lab_own = pltpu.make_async_copy(labels_ref, lab.at[3 - 3 * c], local_sem.at[0])
    lab_own.start()

    def all_start(buf, into, which_sem, sign):
        def step(k, carry):
            pltpu.make_async_remote_copy(
                src_ref=buf.at[k],
                dst_ref=into.at[k],
                send_sem=a2a_send.at[which_sem],
                recv_sem=a2a_recv.at[which_sem],
                device_id=chip_dev(chip + sign * (k + 1)),
                device_id_type=MESH,
            ).start()
            return carry

        lax.fori_loop(0, chips - 1, step, 0)
        own_copy = pltpu.make_async_copy(
            buf.at[chips - 1], into.at[chips - 1], local_sem.at[1 + which_sem]
        )
        own_copy.start()
        return own_copy

    def all_desc(buf, into, which_sem):
        return pltpu.make_async_remote_copy(
            src_ref=buf.at[pl.ds(0, chips - 1)],
            dst_ref=into.at[pl.ds(0, chips - 1)],
            send_sem=a2a_send.at[which_sem],
            recv_sem=a2a_recv.at[which_sem],
            device_id=partner,
            device_id_type=MESH,
        )

    out_own = all_start(send, recv, 0, 1)
    out_all = all_desc(send, recv, 0)
    out_own.wait()
    out_all.wait_recv()

    ids = recv[:, per_chip:, tail:].astype(F32).reshape(rows, LANES).astype(jnp.int32)
    lane = iota((rows, 2 * slots), 1)
    filled = jnp.where(lane < slots, ids[:, :1], ids[:, 1:2] + slots)
    q_t[...] = (filled == lane + 1).astype(F32).astype(BF16)
    ids_t = jnp.transpose(ids.astype(F32)).astype(jnp.int32)
    first = recv[:, :per_chip, :].astype(F32).reshape(rows, width).astype(BF16)
    second = recv[:, per_chip:, :tail].astype(F32).reshape(rows, tail).astype(BF16)
    part_copies = []
    for g in range(2):
        q_mat = (ids_t[g : g + 1, :] == iota((slots, rows), 0) + 1).astype(F32).astype(BF16)
        here = pl.ds(g * slots, slots)
        part[here, :width] = mm(q_mat, first).astype(BF16)
        part[here, width:] = mm(q_mat, second).astype(BF16)
        copy = remote(part.at[here], part_in.at[here], g, partner)
        copy.start()
        part_copies.append(copy)
    lab_own.wait()
    for copy in lab_copies:
        copy.wait()
    for g in range(2):
        part_copies[g].wait()
        here = pl.ds(g * slots, slots)
        home[here, :] = (part[here, :].astype(F32) + part_in[here, :].astype(F32)).astype(BF16)
    half_c = pl.ds(pl.multiple_of(c * half, half), half)
    half_o = pl.ds(pl.multiple_of((1 - c) * half, half), half)

    def ext1(which_half):
        return sl.at[0, which_half]

    ext1_copy = remote(home.at[half_c], ext1(half_c), 2, m_dev(-1))
    ext1_copy.start()
    ext2_copy = remote(home.at[pl.ds(slots, slots)], sl.at[1], 3, m_dev(1 - 2 * c))
    ext2_copy.start()

    factor = scale_ref[0]
    offset = bias_ref[0]

    def slot_rows(o):
        if o < 2:
            return home[o * slots : (o + 1) * slots, :]
        return sl[o - 2]

    def group_terms(o, sums):
        labels = lab[o]

        def chunk(j, sums):
            at = pl.multiple_of(j * t_tile, t_tile)
            inner = mm_nt(text_ref[pl.ds(at, t_tile), :], slot_rows(o))
            logits = factor * inner + offset
            e = jnp.exp(-jnp.abs(logits))
            u = 1.0 + e
            r = 1.0 / u
            log1p = jnp.log(u) + (e - (u - 1.0)) * r
            positive = labels == iota((t_tile, slots), 0) + (d * texts + at)
            sig = jnp.where(logits >= 0.0, r, e * r)
            grad = jnp.where(positive, sig - 1.0, sig)
            loss = jnp.maximum(logits, 0.0) + log1p - jnp.where(positive, logits, 0.0)
            weights = grad.astype(BF16)
            wt[pl.ds(at, t_tile), o * slots : (o + 1) * slots] = weights
            wn[:, pl.ds(at, t_tile)] = jnp.transpose(weights)
            return (
                sums[0] + jnp.sum(loss, axis=0, keepdims=True),
                sums[1] + jnp.sum(grad * inner, axis=0, keepdims=True),
                sums[2] + jnp.sum(grad, axis=0, keepdims=True),
            )

        return lax.fori_loop(0, texts // t_tile, chunk, sums)

    c_tile = 384 if columns % 384 == 0 else LANES

    def image_term(out, base, cast=None):
        def tile(j, carry):
            at = pl.ds(pl.multiple_of(j * c_tile, c_tile), c_tile)
            res = mm(wn[...], text_ref[:, at])
            out[base : base + slots, at] = res if cast is None else res.astype(cast)
            return carry

        lax.fori_loop(0, columns // c_tile, tile, 0)

    sums = (jnp.zeros((1, slots), F32),) * 3
    sums = group_terms(0, sums)
    image_term(own, 0)
    sums = group_terms(1, sums)
    image_term(own, slots)
    own_copy = remote(own, own_in, 4, partner)
    own_copy.start()

    ext1_copy.wait_recv()
    ext1_fwd = remote(ext1(half_c), ext1(half_c), 5, partner)
    ext1_fwd.start()
    ext1_fwd.wait_recv()
    sums = group_terms(2, sums)
    image_term(pre, 0)
    pre_copy = remote(pre.at[half_o], pre_in, 6, partner)
    pre_copy.start()

    ext2_copy.wait_recv()
    sums = group_terms(3, sums)
    image_term(ret2_out, 0, BF16)
    ret2_copy = remote(ret2_out, ret2, 7, m_dev(2 * c - 1))
    ret2_copy.start()

    pre_copy.wait_recv()
    ret1_out[...] = (pre[half_c, :] + pre_in[...]).astype(BF16)
    ret1_copy = remote(ret1_out, ret1.at[half_c], 8, m_dev(1))
    ret1_copy.start()

    lane = iota((8, LANES), 1)
    totals = [jnp.sum(x, axis=1, keepdims=True) for x in sums]
    kind = lax.rem(lane, 3)
    stat[...] = jnp.where(kind == 0, totals[0], jnp.where(kind == 1, totals[1], totals[2]))
    stat_copy = remote(stat, stat_in, 9, partner)
    stat_copy.start()

    n_text = (texts // 2) // t_tile
    text_copies = []

    def text_term(at):
        at = pl.ds(pl.multiple_of(at, t_tile), t_tile)
        res = mm(wt[at, : 2 * slots], home[...])
        res += mm(wt[at, 2 * slots : 3 * slots], sl[0])
        return res + mm(wt[at, 3 * slots :], sl[1])

    for j in range(n_text):
        rows_j = pl.ds(j * t_tile, t_tile)
        text_out[rows_j, :] = text_term((1 - s) * (texts // 2) + j * t_tile).astype(BF16)
        copy = remote(text_out.at[rows_j], text_in.at[rows_j], 15 + j, across)
        copy.start()
        text_copies.append(copy)

    for j in range(n_text):
        gt_ref[j * t_tile : (j + 1) * t_tile, :] = text_term(s * (texts // 2) + j * t_tile)

    ret1_copy.wait_recv()
    ret1_fwd = remote(ret1.at[half_c], ret1.at[half_c], 13, partner)
    ret1_fwd.start()
    ret2_copy.wait_recv()
    ret2_fwd = remote(ret2, ret2b, 14, partner)
    ret2_fwd.start()
    own_copy.wait_recv()
    stat_copy.wait_recv()

    value = stat[...] + stat_in[...]
    top = value.astype(BF16).astype(F32)
    middle = (value - top).astype(BF16).astype(F32)
    low = value - top - middle
    payload = jnp.where(lane < 3, top, jnp.where(lane < 6, middle, jnp.where(lane < 9, low, 0.0)))

    ret1_fwd.wait_recv()
    odd = own[:slots, :] + own_in[:slots, :] + ret1[...].astype(F32)
    slot_grad[:slots, :] = (factor * odd).astype(BF16)
    ret2_fwd.wait_recv()
    evn = own[slots:, :] + own_in[slots:, :] + (ret2[...].astype(F32) + ret2b[...].astype(F32))
    slot_grad[slots:, :] = (factor * evn).astype(BF16)

    payload_rows = jnp.broadcast_to(payload[:per_chip][None], (row_tile // per_chip, per_chip, LANES))
    for r in range(rows // row_tile):
        n = row_tile // per_chip
        q_rows = q_t[r * row_tile : (r + 1) * row_tile, :]
        first = mm(q_rows, slot_grad[:, :width]).reshape(n, per_chip, width)
        second = mm(q_rows, slot_grad[:, width:]).reshape(n, per_chip, tail)
        second = jnp.concatenate([second, payload_rows], axis=2)
        back[r * n : (r + 1) * n] = jnp.concatenate([first, second], axis=1).astype(BF16)

    back_own = all_start(back, back_recv, 1, -1)
    back_all = all_desc(back, back_recv, 1)
    for j in range(n_text):
        text_copies[j].wait_recv()
        rows_j = pl.ds(j * t_tile, t_tile)
        gt_ref[rows_j, :] = factor * (gt_ref[rows_j, :] + text_in[rows_j, :].astype(F32))
    back_own.wait()
    back_all.wait_recv()

    first = back_recv[:, :per_chip, :].astype(F32).reshape(rows, width).astype(BF16)
    second = back_recv[:, per_chip:, :tail].astype(F32).reshape(rows, tail).astype(BF16)
    for r in range(rows // row_tile):
        at = slice(r * row_tile, (r + 1) * row_tile)
        p_rows = p_t[at, :]
        gi_ref[at, :width] = mm(p_rows, first).astype(BF16)
        gi_ref[at, width:] = mm(p_rows, second).astype(BF16)

    sums_in = back_recv[:, per_chip:, tail:].astype(F32)[:, 0, :].astype(BF16)
    source = (chip + 1 + iota((chips, chips), 1)) & (chips - 1)
    order = (source == iota((chips, chips), 0)).astype(F32).astype(BF16)
    total = jnp.sum(mm(order, sums_in), axis=0, keepdims=True)
    lane = iota((1, LANES), 1)
    for k, ref in enumerate((loss_ref, gscale_ref, gbias_ref)):
        picked = (lane < 9) & (lax.rem(lane, 3) == k)
        ref[0] = jnp.sum(jnp.where(picked, total, 0.0)) / pairs

    out_all.wait_send()
    back_all.wait_send()
    for copy in (
        ext1_copy,
        ext2_copy,
        own_copy,
        ext1_fwd,
        pre_copy,
        ret2_copy,
        ret1_copy,
        stat_copy,
        ret1_fwd,
        ret2_fwd,
        *text_copies,
    ):
        copy.wait_send()


def local(images, text_embeds, dest_slot, labels, logit_scale, logit_bias):
    n_dp = lax.axis_size("dp")
    rows, columns = images.shape
    texts = text_embeds.shape[0]
    slots = labels.shape[0]
    chips = n_dp
    per_chip = rows // chips
    width = (columns + LANES) // 2
    pairs = float(slots * n_dp * 2 * STOPS * texts)
    vmem = pl.BlockSpec(memory_space=pltpu.VMEM)
    smem = pl.BlockSpec(memory_space=pltpu.SMEM)
    message = pltpu.VMEM((chips, 2 * per_chip, width), BF16)

    def buf(n, dtype=BF16):
        return pltpu.VMEM((n, columns), dtype)

    scalar = jax.ShapeDtypeStruct((1,), F32)
    return pl.pallas_call(
        functools.partial(kernel, n_dp, pairs),
        out_shape=(
            jax.ShapeDtypeStruct((rows, columns), BF16),
            jax.ShapeDtypeStruct((texts // 2, columns), F32),
            scalar,
            scalar,
            scalar,
        ),
        in_specs=[smem, smem, vmem, vmem, vmem, vmem],
        out_specs=(vmem, vmem, smem, smem, smem),
        scratch_shapes=[
            message,
            message,
            message,
            message,
            buf(2 * slots),
            buf(2 * slots),
            buf(2 * slots),
            pltpu.VMEM((2, slots, columns), BF16),
            pltpu.VMEM((4, 1, slots), jnp.int32),
            pltpu.VMEM((texts, 4 * slots), BF16),
            pltpu.VMEM((slots, texts), BF16),
            buf(2 * slots, F32),
            buf(2 * slots, F32),
            buf(slots, F32),
            buf(slots // 2, F32),
            buf(slots // 2),
            buf(slots),
            buf(slots),
            buf(slots),
            buf(slots),
            buf(2 * slots),
            buf(texts // 2),
            buf(texts // 2),
            pltpu.VMEM((rows, rows), BF16),
            pltpu.VMEM((rows, 2 * slots), BF16),
            pltpu.VMEM((8, LANES), F32),
            pltpu.VMEM((8, LANES), F32),
            pltpu.SemaphoreType.DMA((2,)),
            pltpu.SemaphoreType.DMA((2,)),
            pltpu.SemaphoreType.DMA((3,)),
            pltpu.SemaphoreType.DMA((24,)),
            pltpu.SemaphoreType.DMA((24,)),
        ],
        compiler_params=pltpu.CompilerParams(
            collective_id=0,
            has_side_effects=True,
            vmem_limit_bytes=58 * 1024 * 1024,
        ),
    )(
        logit_scale,
        logit_bias,
        dest_slot.reshape(1, rows),
        labels.reshape(1, slots),
        images,
        text_embeds,
    )


def solution(mesh):
    return jax.shard_map(
        local,
        mesh=mesh,
        in_specs=(
            P(("dp", "sub"), None),
            P("dp", None),
            P(("dp", "sub")),
            P(("dp", "sub")),
            P(),
            P(),
        ),
        out_specs=(P(("dp", "sub"), None), P(("dp", "sub"), None), P(), P(), P()),
        check_vma=False,
    )
```

```python
import functools

import jax
import jax.numpy as jnp
from jax import lax
from jax.experimental import pallas as pl
from jax.experimental.pallas import tpu as pltpu
from jax.sharding import PartitionSpec as P

STOPS = 4
LANES = 128
MESH = pl.DeviceIdType.MESH
F32 = jnp.float32
BF16 = jnp.bfloat16


def iota(shape, axis):
    return lax.broadcasted_iota(jnp.int32, shape, axis)


def mm(a, b):
    return lax.dot_general(a, b, (((1,), (0,)), ((), ())), preferred_element_type=F32)


def mm_nt(a, b):
    return lax.dot_general(a, b, (((1,), (1,)), ((), ())), preferred_element_type=F32)


def kernel(
    n_dp,
    scale_ref,
    bias_ref,
    dest_ref,
    labels_ref,
    images_ref,
    text_hbm,
    back_recv,
    text_in,
    gt_hbm,
    p_hbm,
    text_ref,
    send,
    recv,
    back,
    home,
    part,
    part_in,
    sl,
    lab,
    wt,
    wn,
    own,
    own_in,
    pre,
    pre_in,
    ret1_out,
    ret1,
    ret2_out,
    ret2,
    ret2b,
    slot_grad,
    text_sum,
    text_out,
    gt,
    p_t,
    q_t,
    stat,
    stat_in,
    a2a_send,
    a2a_recv,
    local_sem,
    ss,
    rs,
):
    rows, columns = images_ref.shape
    texts = text_ref.shape[0]
    text_half = texts // 2
    slots = labels_ref.shape[1]
    half = slots // 2
    chips = n_dp
    n_m = n_dp // 2
    per_chip = rows // chips
    width = send.shape[2]
    tail = columns - width
    t_tile = min(256, texts // 2)

    d = lax.axis_index("dp")
    s = lax.axis_index("sub")
    m = lax.div(d, 2)
    c = lax.rem(d, 2)
    chip = m * 2 + s
    partner = (m * 2 + (1 - c), s)
    across = (d, 1 - s)

    def chip_dev(i):
        i = lax.rem(i + chips, chips)
        return (lax.div(i, 2) * 2 + c, lax.rem(i, 2))

    def m_dev(step):
        return (lax.rem(m + step + n_m, n_m) * 2 + c, s)

    def dp_dev(step):
        return (lax.rem(d + step + n_dp, n_dp), s)

    text_copy = pltpu.make_async_copy(text_hbm, text_ref, local_sem.at[3])
    text_copy.start()

    barrier = pltpu.get_barrier_semaphore()

    def greet(k, carry):
        pl.semaphore_signal(barrier, inc=1, device_id=chip_dev(chip + k), device_id_type=MESH)
        return carry

    lax.fori_loop(1, chips, greet, 0)
    for dev in (partner, dp_dev(1), dp_dev(3)):
        pl.semaphore_signal(barrier, inc=1, device_id=dev, device_id_type=MESH)

    def remote(src, dst, k, dev):
        return pltpu.make_async_remote_copy(
            src_ref=src,
            dst_ref=dst,
            send_sem=ss.at[k],
            recv_sem=rs.at[k],
            device_id=dev,
            device_id_type=MESH,
        )

    q = dest_ref[...]
    valid = q >= 0
    group = lax.div(jnp.maximum(q, 0), 2 * slots)
    rest = jnp.maximum(q, 0) - group * (2 * slots)
    to_sub = lax.div(rest, slots)
    slot_id = rest - to_sub * slots
    even = (group & 1) == 0
    to_m = lax.div((group + (n_dp - 1)) & (n_dp - 1), 2)
    rel = (to_m * 2 + to_sub - chip + (chips - 1)) & (chips - 1)
    rel = jnp.where(valid, rel, -1)
    onehot = rel == iota((chips, rows), 0)
    earlier = (iota((rows, rows), 0) < iota((rows, rows), 1)).astype(F32).astype(BF16)
    onehot_f = onehot.astype(F32)
    rank = mm(onehot_f.astype(BF16), earlier)
    within = jnp.sum(onehot_f * rank, axis=0, keepdims=True)
    placed = jnp.where(valid, rel.astype(F32) * float(per_chip) + within, -1.0)
    placed_col = jnp.transpose(jnp.broadcast_to(placed, (LANES, rows)))[:, :1].astype(jnp.int32)
    p_t[...] = (placed_col == iota((rows, rows), 1)).astype(F32).astype(BF16)
    p_copy = pltpu.make_async_copy(p_t, p_hbm, local_sem.at[4])
    p_copy.start()
    placed_int = placed.astype(jnp.int32)
    id_plus = (slot_id + 1).astype(F32)
    id_odd = jnp.where(valid & jnp.logical_not(even), id_plus, 0.0)
    id_even = jnp.where(valid & even, id_plus, 0.0)
    which = iota((LANES, rows), 0)
    id_rows = jnp.where(which == 0, id_odd, jnp.where(which == 1, id_even, 0.0))
    ids_block = jnp.transpose(id_rows).astype(BF16)
    row_tile = min(128, rows)
    for r in range(rows // row_tile):
        p_mat = (placed_int == iota((row_tile, rows), 0) + r * row_tile).astype(F32).astype(BF16)
        n = row_tile // per_chip
        first = mm(p_mat, images_ref[:, :width]).reshape(n, per_chip, width)
        second = mm(p_mat, images_ref[:, width:]).reshape(n, per_chip, tail)
        third = mm(p_mat, ids_block).reshape(n, per_chip, LANES)
        second = jnp.concatenate([second, third], axis=2)
        send[r * n : (r + 1) * n] = jnp.concatenate([first, second], axis=1).astype(BF16)

    pl.semaphore_wait(barrier, chips - 1 + 3)

    lab_copies = [
        remote(labels_ref, lab.at[slot], 9 + step, dp_dev(-step))
        for step, slot in ((1, 1 - c), (2, 1 + c), (3, 3 - c))
    ]
    for copy in lab_copies:
        copy.start()
    lab_own = pltpu.make_async_copy(labels_ref, lab.at[3 - 3 * c], local_sem.at[0])
    lab_own.start()

    def all_start(buf, into, which_sem, sign, lo, hi):
        def step(k, carry):
            pltpu.make_async_remote_copy(
                src_ref=buf.at[k],
                dst_ref=into.at[k],
                send_sem=a2a_send.at[which_sem],
                recv_sem=a2a_recv.at[which_sem],
                device_id=chip_dev(chip + sign * (k + 1)),
                device_id_type=MESH,
            ).start()
            return carry

        lax.fori_loop(lo, min(hi, chips - 1), step, 0)

    def own_start(buf, into, which_sem):
        copy = pltpu.make_async_copy(
            buf.at[chips - 1], into.at[chips - 1], local_sem.at[1 + which_sem]
        )
        copy.start()
        return copy

    def all_desc(buf, into, which_sem):
        return pltpu.make_async_remote_copy(
            src_ref=buf.at[pl.ds(0, chips - 1)],
            dst_ref=into.at[pl.ds(0, chips - 1)],
            send_sem=a2a_send.at[which_sem],
            recv_sem=a2a_recv.at[which_sem],
            device_id=partner,
            device_id_type=MESH,
        )

    all_start(send, recv, 0, 1, 0, chips)
    out_own = own_start(send, recv, 0)
    out_all = all_desc(send, recv, 0)
    out_own.wait()
    out_all.wait_recv()

    ids = recv[:, per_chip:, tail:].astype(F32).reshape(rows, LANES).astype(jnp.int32)
    lane = iota((rows, 2 * slots), 1)
    filled = jnp.where(lane < slots, ids[:, :1], ids[:, 1:2] + slots)
    q_t[...] = (filled == lane + 1).astype(F32).astype(BF16)
    ids_t = jnp.transpose(ids.astype(F32)).astype(jnp.int32)
    first = recv[:, :per_chip, :].astype(F32).reshape(rows, width).astype(BF16)
    second = recv[:, per_chip:, :tail].astype(F32).reshape(rows, tail).astype(BF16)
    part_copies = []
    for g in range(2):
        q_mat = (ids_t[g : g + 1, :] == iota((slots, rows), 0) + 1).astype(F32).astype(BF16)
        here = pl.ds(g * slots, slots)
        part[here, :width] = mm(q_mat, first).astype(BF16)
        part[here, width:] = mm(q_mat, second).astype(BF16)
        copy = remote(part.at[here], part_in.at[here], g, partner)
        copy.start()
        part_copies.append(copy)
    lab_own.wait()
    for copy in lab_copies:
        copy.wait()
    for g in range(2):
        part_copies[g].wait()
        here = pl.ds(g * slots, slots)
        home[here, :] = (part[here, :].astype(F32) + part_in[here, :].astype(F32)).astype(BF16)
    half_c = pl.ds(pl.multiple_of(c * half, half), half)
    half_o = pl.ds(pl.multiple_of((1 - c) * half, half), half)

    def ext1(which_half):
        return sl.at[0, which_half]

    ext1_copy = remote(home.at[half_c], ext1(half_c), 2, m_dev(-1))
    ext1_copy.start()
    ext2_copy = remote(home.at[pl.ds(slots, slots)], sl.at[1], 3, m_dev(1 - 2 * c))

    @pl.when(c == 0)
    def _():
        ext2_copy.start()

    text_copy.wait()

    factor = scale_ref[...]
    offset = bias_ref[...]

    def slot_rows(o):
        if o < 2:
            return home[o * slots : (o + 1) * slots, :]
        return sl[o - 2]

    def group_terms(o, sums):
        labels = lab[o]

        def chunk(j, sums):
            at = pl.multiple_of(j * t_tile, t_tile)
            inner = mm_nt(text_ref[pl.ds(at, t_tile), :], slot_rows(o))
            logits = factor * inner + offset
            e = jnp.exp(-jnp.abs(logits))
            u = 1.0 + e
            r = 1.0 / u
            log1p = jnp.log(u) + (e - (u - 1.0)) * r
            positive = labels == iota((t_tile, slots), 0) + (d * texts + at)
            sig = jnp.where(logits >= 0.0, r, e * r)
            grad = jnp.where(positive, sig - 1.0, sig)
            loss = jnp.maximum(logits, 0.0) + log1p - jnp.where(positive, logits, 0.0)
            weights = grad.astype(BF16)
            wt[pl.ds(at, t_tile), o * slots : (o + 1) * slots] = weights
            wn[o, :, pl.ds(at, t_tile)] = jnp.transpose(weights)
            return (
                sums[0] + jnp.sum(loss, axis=0, keepdims=True),
                sums[1] + jnp.sum(grad * inner, axis=0, keepdims=True),
                sums[2] + jnp.sum(grad, axis=0, keepdims=True),
            )

        return lax.fori_loop(0, texts // t_tile, chunk, sums)

    c_tile = 384 if columns % 384 == 0 else LANES

    def image_term(out, base, o, cast=None):
        def tile(j, carry):
            at = pl.ds(pl.multiple_of(j * c_tile, c_tile), c_tile)
            res = mm(wn[o], text_ref[:, at])
            out[base : base + slots, at] = res if cast is None else res.astype(cast)
            return carry

        lax.fori_loop(0, columns // c_tile, tile, 0)

    n_text = text_half // t_tile

    def text_rows(base, j):
        return pl.ds(pl.multiple_of(base + j * t_tile, t_tile), t_tile)

    def text_part(base, j, first, last, rows_of):
        return mm(wt[text_rows(base, j), first * slots : last * slots], rows_of())

    mine, theirs = s * text_half, (1 - s) * text_half

    sums = (jnp.zeros((1, slots), F32),) * 3
    sums = group_terms(0, sums)
    sums = group_terms(1, sums)

    @pl.when(c == 1)
    def _():
        ext2_copy.start()

    image_term(own, 0, 0)
    image_term(own, slots, 1)
    own_copy = remote(own, own_in, 4, partner)
    own_copy.start()
    for j in range(n_text):
        here = pl.ds(j * t_tile, t_tile)
        text_sum[here, :] = text_part(theirs, j, 0, 2, lambda: home[...])

    ext1_copy.wait_recv()
    ext1_fwd = remote(ext1(half_c), ext1(half_c), 5, partner)
    ext1_fwd.start()
    for j in range(n_text):
        here = pl.ds(j * t_tile, t_tile)
        gt[here, :] = text_part(mine, j, 0, 2, lambda: home[...])
    ext1_fwd.wait_recv()
    sums = group_terms(2, sums)
    image_term(pre, 0, 2)
    pre_copy = remote(pre.at[half_o], pre_in, 6, partner)
    pre_copy.start()
    for j in range(n_text):
        here = pl.ds(j * t_tile, t_tile)
        text_sum[here, :] += text_part(theirs, j, 2, 3, lambda: sl[0])
    pre_copy.wait_recv()
    ret1_out[...] = (pre[half_c, :] + pre_in[...]).astype(BF16)
    ret1_copy = remote(ret1_out, ret1.at[half_c], 8, m_dev(1))
    ret1_copy.start()

    ext2_copy.wait_recv()
    sums = group_terms(3, sums)
    text_copies = []

    def send_text(j):
        here = pl.ds(j * t_tile, t_tile)
        text_out[here, :] = (
            text_sum[here, :] + text_part(theirs, j, 3, 4, lambda: sl[1])
        ).astype(BF16)
        copy = remote(text_out.at[here], text_in.at[here], 15 + j, across)
        copy.start()
        text_copies.append(copy)

    send_text(0)
    image_term(ret2_out, 0, 3, BF16)
    ret2_copy = remote(ret2_out, ret2, 7, m_dev(2 * c - 1))
    ret2_copy.start()
    for j in range(1, n_text):
        send_text(j)

    lane = iota((8, LANES), 1)
    totals = [jnp.sum(x, axis=1, keepdims=True) for x in sums]
    kind = lax.rem(lane, 3)
    stat[...] = jnp.where(kind == 0, totals[0], jnp.where(kind == 1, totals[1], totals[2]))
    stat_copy = remote(stat, stat_in, 9, partner)
    stat_copy.start()

    for j in range(n_text):
        here = pl.ds(j * t_tile, t_tile)
        gt[here, :] += text_part(mine, j, 2, 3, lambda: sl[0]) + text_part(
            mine, j, 3, 4, lambda: sl[1]
        )
    gt_copy = pltpu.make_async_copy(gt, gt_hbm, local_sem.at[5])
    gt_copy.start()

    ret1_copy.wait_recv()
    ret1_fwd = remote(ret1.at[half_c], ret1.at[half_c], 13, partner)
    ret1_fwd.start()
    ret2_copy.wait_recv()
    ret2_fwd = remote(ret2, ret2b, 14, partner)
    ret2_fwd.start()
    own_copy.wait_recv()
    stat_copy.wait_recv()

    value = stat[...] + stat_in[...]
    top = value.astype(BF16).astype(F32)
    middle = (value - top).astype(BF16).astype(F32)
    low = value - top - middle
    payload = jnp.where(lane < 3, top, jnp.where(lane < 6, middle, jnp.where(lane < 9, low, 0.0)))

    ret1_fwd.wait_recv()
    odd = own[:slots, :] + own_in[:slots, :] + ret1[...].astype(F32)
    slot_grad[:slots, :] = (factor * odd).astype(BF16)
    ret2_fwd.wait_recv()
    evn = own[slots:, :] + own_in[slots:, :] + (ret2[...].astype(F32) + ret2b[...].astype(F32))
    slot_grad[slots:, :] = (factor * evn).astype(BF16)

    payload_rows = jnp.broadcast_to(payload[:per_chip][None], (row_tile // per_chip, per_chip, LANES))
    for r in range(rows // row_tile):
        n = row_tile // per_chip
        q_rows = q_t[r * row_tile : (r + 1) * row_tile, :]
        first = mm(q_rows, slot_grad[:, :width]).reshape(n, per_chip, width)
        second = mm(q_rows, slot_grad[:, width:]).reshape(n, per_chip, tail)
        second = jnp.concatenate([second, payload_rows], axis=2)
        back[r * n : (r + 1) * n] = jnp.concatenate([first, second], axis=1).astype(BF16)
        all_start(back, back_recv, 1, -1, r * n, (r + 1) * n)

    back_own = own_start(back, back_recv, 1)
    back_all = all_desc(back, back_recv, 1)
    for copy in text_copies:
        copy.wait_recv()
    p_copy.wait()
    gt_copy.wait()
    back_own.wait()
    back_all.wait_recv()

    out_all.wait_send()
    back_all.wait_send()
    for copy in (
        ext1_copy,
        ext2_copy,
        own_copy,
        ext1_fwd,
        pre_copy,
        ret2_copy,
        ret1_copy,
        stat_copy,
        ret1_fwd,
        ret2_fwd,
        *text_copies,
    ):
        copy.wait_send()


def finish(n_dp, pairs, per_chip, scale_ref, back_ref, text_in_ref, gt_in_ref, p_ref, *rest):
    gi_ref, gt_ref, loss_ref, gscale_ref, gbias_ref, rows_in = rest
    chips, _, width = back_ref.shape
    rows, columns = rows_in.shape
    tail = columns - width

    @pl.when(pl.program_id(0) == 0)
    def _():
        rows_in[:, :width] = (
            back_ref[:, :per_chip, :].astype(F32).reshape(rows, width).astype(BF16)
        )
        rows_in[:, width:] = (
            back_ref[:, per_chip:, :tail].astype(F32).reshape(rows, tail).astype(BF16)
        )
        chip = lax.div(lax.axis_index("dp"), 2) * 2 + lax.axis_index("sub")
        sums_in = back_ref[:, per_chip:, tail:].astype(F32)[:, 0, :].astype(BF16)
        source = (chip + 1 + iota((chips, chips), 1)) & (chips - 1)
        order = (source == iota((chips, chips), 0)).astype(F32).astype(BF16)
        total = jnp.sum(mm(order, sums_in), axis=0, keepdims=True)
        lane = iota((1, LANES), 1)
        for k, ref in enumerate((loss_ref, gscale_ref, gbias_ref)):
            picked = (lane < 9) & (lax.rem(lane, 3) == k)
            ref[0] = jnp.sum(jnp.where(picked, total, 0.0)) / pairs

    gi_ref[...] = mm(p_ref[...], rows_in[...]).astype(BF16)
    gt_ref[...] = scale_ref[...] * (gt_in_ref[...] + text_in_ref[...].astype(F32))


def local(images, text_embeds, dest_slot, labels, logit_scale, logit_bias):
    n_dp = lax.axis_size("dp")
    rows, columns = images.shape
    texts = text_embeds.shape[0]
    slots = labels.shape[0]
    chips = n_dp
    per_chip = rows // chips
    width = (columns + LANES) // 2
    pairs = float(slots * n_dp * 2 * STOPS * texts)
    vmem = pl.BlockSpec(memory_space=pltpu.VMEM)
    smem = pl.BlockSpec(memory_space=pltpu.SMEM)
    hbm = pl.BlockSpec(memory_space=pl.ANY)
    message = pltpu.VMEM((chips, 2 * per_chip, width), BF16)

    def buf(n, dtype=BF16):
        return pltpu.VMEM((n, columns), dtype)

    scale = logit_scale.reshape(1, 1)
    back, text_in, gt, p_t = pl.pallas_call(
        functools.partial(kernel, n_dp),
        out_shape=(
            jax.ShapeDtypeStruct((chips, 2 * per_chip, width), BF16),
            jax.ShapeDtypeStruct((texts // 2, columns), BF16),
            jax.ShapeDtypeStruct((texts // 2, columns), F32),
            jax.ShapeDtypeStruct((rows, rows), BF16),
        ),
        in_specs=[vmem, vmem, vmem, vmem, vmem, hbm],
        out_specs=(hbm, hbm, hbm, hbm),
        scratch_shapes=[
            buf(texts),
            message,
            message,
            message,
            buf(2 * slots),
            buf(2 * slots),
            buf(2 * slots),
            pltpu.VMEM((2, slots, columns), BF16),
            pltpu.VMEM((4, 1, slots), jnp.int32),
            pltpu.VMEM((texts, 4 * slots), BF16),
            pltpu.VMEM((4, slots, texts), BF16),
            buf(2 * slots, F32),
            buf(2 * slots, F32),
            buf(slots, F32),
            buf(slots // 2, F32),
            buf(slots // 2),
            buf(slots),
            buf(slots),
            buf(slots),
            buf(slots),
            buf(2 * slots),
            buf(texts // 2, F32),
            buf(texts // 2),
            buf(texts // 2, F32),
            pltpu.VMEM((rows, rows), BF16),
            pltpu.VMEM((rows, 2 * slots), BF16),
            pltpu.VMEM((8, LANES), F32),
            pltpu.VMEM((8, LANES), F32),
            pltpu.SemaphoreType.DMA((2,)),
            pltpu.SemaphoreType.DMA((2,)),
            pltpu.SemaphoreType.DMA((6,)),
            pltpu.SemaphoreType.DMA((24,)),
            pltpu.SemaphoreType.DMA((24,)),
        ],
        compiler_params=pltpu.CompilerParams(
            collective_id=0,
            has_side_effects=True,
            vmem_limit_bytes=58 * 1024 * 1024,
        ),
    )(
        scale,
        logit_bias.reshape(1, 1),
        dest_slot.reshape(1, rows),
        labels.reshape(1, slots),
        images,
        text_embeds,
    )
    tiles = 4
    tile_rows = pl.BlockSpec((rows // tiles, columns), lambda i: (i, 0))
    tile_texts = pl.BlockSpec((texts // 2 // tiles, columns), lambda i: (i, 0))
    scalar = jax.ShapeDtypeStruct((1,), F32)
    return pl.pallas_call(
        functools.partial(finish, n_dp, pairs, per_chip),
        out_shape=(
            jax.ShapeDtypeStruct((rows, columns), BF16),
            jax.ShapeDtypeStruct((texts // 2, columns), F32),
            scalar,
            scalar,
            scalar,
        ),
        grid=(tiles,),
        in_specs=[
            pl.BlockSpec((1, 1), lambda i: (0, 0)),
            pl.BlockSpec(back.shape, lambda i: (0, 0, 0)),
            tile_texts,
            tile_texts,
            pl.BlockSpec((rows // tiles, rows), lambda i: (i, 0)),
        ],
        out_specs=(tile_rows, tile_texts, smem, smem, smem),
        scratch_shapes=[buf(rows)],
        compiler_params=pltpu.CompilerParams(vmem_limit_bytes=40 * 1024 * 1024),
    )(scale, back, text_in, gt, p_t)


def solution(mesh):
    return jax.shard_map(
        local,
        mesh=mesh,
        in_specs=(
            P(("dp", "sub"), None),
            P("dp", None),
            P(("dp", "sub")),
            P(("dp", "sub")),
            P(),
            P(),
        ),
        out_specs=(P(("dp", "sub"), None), P(("dp", "sub"), None), P(), P(), P()),
        check_vma=False,
    )
```

```python
import functools

import jax
import jax.numpy as jnp
from jax import lax
from jax.experimental import pallas as pl
from jax.experimental.pallas import tpu as pltpu
from jax.sharding import PartitionSpec as P

STOPS = 4
LANES = 128
MESH = pl.DeviceIdType.MESH
STRIDE, UNSTRIDE = 27, 19
LOG2E = 1.4426950408889634
LN2 = 0.6931471805599453
F32 = jnp.float32
BF16 = jnp.bfloat16


def iota(shape, axis):
    return lax.broadcasted_iota(jnp.int32, shape, axis)


def mm(a, b):
    return lax.dot_general(a, b, (((1,), (0,)), ((), ())), preferred_element_type=F32)


def mm_tn(a, b):
    return lax.dot_general(a, b, (((0,), (0,)), ((), ())), preferred_element_type=F32)


def fold(x, op):
    while x.shape[0] > 8:
        n = x.shape[0] // 2
        x = op(x[:n], x[n:])
    return x


def mm_nt(a, b):
    return lax.dot_general(a, b, (((1,), (1,)), ((), ())), preferred_element_type=F32)


def kernel(
    n_dp,
    scale_ref,
    bias_ref,
    dest_ref,
    labels_ref,
    images_ref,
    text_hbm,
    back_recv,
    text_in,
    gt_hbm,
    p_hbm,
    text_ref,
    send,
    recv,
    back,
    home,
    part,
    part_in,
    sl,
    lab,
    wt,
    inner_ref,
    sums_ref,
    own,
    own_in,
    pre,
    pre_in,
    ret1_out,
    ret1,
    ret2_out,
    ret2,
    ret2b,
    slot_grad,
    text_sum,
    text_out,
    gt,
    p_t,
    q_t,
    stat,
    stat_in,
    a2a_send,
    a2a_recv,
    local_sem,
    ss,
    rs,
):
    rows, columns = images_ref.shape
    texts = text_ref.shape[0]
    text_half = texts // 2
    slots = labels_ref.shape[1]
    half = slots // 2
    chips = n_dp
    n_m = n_dp // 2
    per_chip = rows // chips
    width = send.shape[2]
    tail = columns - width
    t_tile = min(256, texts // 2)

    d = lax.axis_index("dp")
    s = lax.axis_index("sub")
    m = lax.div(d, 2)
    c = lax.rem(d, 2)
    chip = m * 2 + s
    partner = (m * 2 + (1 - c), s)
    across = (d, 1 - s)

    def chip_dev(i):
        i = lax.rem(i + chips, chips)
        return (lax.div(i, 2) * 2 + c, lax.rem(i, 2))

    def m_dev(step):
        return (lax.rem(m + step + n_m, n_m) * 2 + c, s)

    def dp_dev(step):
        return (lax.rem(d + step + n_dp, n_dp), s)

    text_copy = pltpu.make_async_copy(text_hbm, text_ref, local_sem.at[3])
    text_copy.start()

    barrier = pltpu.get_barrier_semaphore()

    def greet(k, carry):
        pl.semaphore_signal(barrier, inc=1, device_id=chip_dev(chip + k), device_id_type=MESH)
        return carry

    lax.fori_loop(1, chips, greet, 0)
    for dev in (partner, dp_dev(1), dp_dev(3)):
        pl.semaphore_signal(barrier, inc=1, device_id=dev, device_id_type=MESH)

    def remote(src, dst, k, dev):
        return pltpu.make_async_remote_copy(
            src_ref=src,
            dst_ref=dst,
            send_sem=ss.at[k],
            recv_sem=rs.at[k],
            device_id=dev,
            device_id_type=MESH,
        )

    q = dest_ref[...]
    valid = q >= 0
    group = lax.div(jnp.maximum(q, 0), 2 * slots)
    rest = jnp.maximum(q, 0) - group * (2 * slots)
    to_sub = lax.div(rest, slots)
    slot_id = rest - to_sub * slots
    even = (group & 1) == 0
    to_m = lax.div((group + (n_dp - 1)) & (n_dp - 1), 2)
    rel = ((to_m * 2 + to_sub - chip + chips) * UNSTRIDE + (chips - 1)) & (chips - 1)
    rel = jnp.where(valid, rel, -1)
    onehot = rel == iota((chips, rows), 0)
    earlier = (iota((rows, rows), 0) < iota((rows, rows), 1)).astype(F32).astype(BF16)
    onehot_f = onehot.astype(F32)
    rank = mm(onehot_f.astype(BF16), earlier)
    within = jnp.sum(onehot_f * rank, axis=0, keepdims=True)
    placed = jnp.where(valid, rel.astype(F32) * float(per_chip) + within, -1.0)
    placed_col = jnp.transpose(jnp.broadcast_to(placed, (LANES, rows)))[:, :1].astype(jnp.int32)
    p_t[...] = (placed_col == iota((rows, rows), 1)).astype(F32).astype(BF16)
    p_copy = pltpu.make_async_copy(p_t, p_hbm, local_sem.at[4])
    p_copy.start()
    placed_int = placed.astype(jnp.int32)
    id_plus = (slot_id + 1).astype(F32)
    id_odd = jnp.where(valid & jnp.logical_not(even), id_plus, 0.0)
    id_even = jnp.where(valid & even, id_plus, 0.0)
    which = iota((LANES, rows), 0)
    id_rows = jnp.where(which == 0, id_odd, jnp.where(which == 1, id_even, 0.0))
    ids_block = jnp.transpose(id_rows).astype(BF16)
    row_tile = min(128, rows)
    for r in range(rows // row_tile):
        p_mat = (placed_int == iota((row_tile, rows), 0) + r * row_tile).astype(F32).astype(BF16)
        n = row_tile // per_chip
        first = mm(p_mat, images_ref[:, :width]).reshape(n, per_chip, width)
        second = mm(p_mat, images_ref[:, width:]).reshape(n, per_chip, tail)
        third = mm(p_mat, ids_block).reshape(n, per_chip, LANES)
        second = jnp.concatenate([second, third], axis=2)
        send[r * n : (r + 1) * n] = jnp.concatenate([first, second], axis=1).astype(BF16)

    pl.semaphore_wait(barrier, chips - 1 + 3)

    lab_copies = [
        remote(labels_ref, lab.at[slot], 9 + step, dp_dev(-step))
        for step, slot in ((1, 1 - c), (2, 1 + c), (3, 3 - c))
    ]
    for copy in lab_copies:
        copy.start()
    lab_own = pltpu.make_async_copy(labels_ref, lab.at[3 - 3 * c], local_sem.at[0])
    lab_own.start()

    def all_start(buf, into, which_sem, sign, lo, hi):
        def step(k, carry):
            pltpu.make_async_remote_copy(
                src_ref=buf.at[k],
                dst_ref=into.at[k],
                send_sem=a2a_send.at[which_sem],
                recv_sem=a2a_recv.at[which_sem],
                device_id=chip_dev(chip + sign * lax.rem((k + 1) * STRIDE, chips)),
                device_id_type=MESH,
            ).start()
            return carry

        lax.fori_loop(lo, min(hi, chips - 1), step, 0)

    def own_start(buf, into, which_sem):
        copy = pltpu.make_async_copy(
            buf.at[chips - 1], into.at[chips - 1], local_sem.at[1 + which_sem]
        )
        copy.start()
        return copy

    def all_desc(buf, into, which_sem):
        return pltpu.make_async_remote_copy(
            src_ref=buf.at[pl.ds(0, chips - 1)],
            dst_ref=into.at[pl.ds(0, chips - 1)],
            send_sem=a2a_send.at[which_sem],
            recv_sem=a2a_recv.at[which_sem],
            device_id=partner,
            device_id_type=MESH,
        )

    all_start(send, recv, 0, 1, 0, chips)
    out_own = own_start(send, recv, 0)
    out_all = all_desc(send, recv, 0)
    out_own.wait()
    out_all.wait_recv()

    ids = recv[:, per_chip:, tail:].astype(F32).reshape(rows, LANES).astype(jnp.int32)
    lane = iota((rows, 2 * slots), 1)
    filled = jnp.where(lane < slots, ids[:, :1], ids[:, 1:2] + slots)
    q_t[...] = (filled == lane + 1).astype(F32).astype(BF16)
    ids_t = jnp.transpose(ids.astype(F32)).astype(jnp.int32)
    first = recv[:, :per_chip, :].astype(F32).reshape(rows, width).astype(BF16)
    second = recv[:, per_chip:, :tail].astype(F32).reshape(rows, tail).astype(BF16)
    part_copies = []
    for g in range(2):
        q_mat = (ids_t[g : g + 1, :] == iota((slots, rows), 0) + 1).astype(F32).astype(BF16)
        here = pl.ds(g * slots, slots)
        part[here, :width] = mm(q_mat, first).astype(BF16)
        part[here, width:] = mm(q_mat, second).astype(BF16)
        copy = remote(part.at[here], part_in.at[here], g, partner)
        copy.start()
        part_copies.append(copy)
    lab_own.wait()
    for copy in lab_copies:
        copy.wait()
    for g in range(2):
        part_copies[g].wait()
        here = pl.ds(g * slots, slots)
        home[here, :] = (part[here, :].astype(F32) + part_in[here, :].astype(F32)).astype(BF16)
    half_c = pl.ds(pl.multiple_of(c * half, half), half)
    half_o = pl.ds(pl.multiple_of((1 - c) * half, half), half)

    def ext1(which_half):
        return sl.at[which_half]

    ext1_copy = remote(home.at[half_c], ext1(half_c), 2, m_dev(-1))
    ext1_copy.start()
    ext2_copy = remote(home.at[pl.ds(slots, slots)], sl.at[pl.ds(slots, slots)], 3, m_dev(1 - 2 * c))

    @pl.when(c == 0)
    def _():
        ext2_copy.start()

    text_copy.wait()

    factor = scale_ref[...]
    factor2 = factor * LOG2E
    offset2 = bias_ref[...] * LOG2E
    sums_ref[...] = jnp.zeros_like(sums_ref)

    def add(x, y):
        return x + y

    def scores(o, n, slot_rows):
        wide = n * slots
        inner_ref[:, :wide] = mm_nt(text_ref[...], slot_rows)
        labels = lab[o] if n == 1 else jnp.concatenate([lab[o], lab[o + 1]], axis=1)

        def chunk(j, sums):
            at = pl.multiple_of(j * t_tile, t_tile)
            inner = inner_ref[pl.ds(at, t_tile), :wide]
            logits = factor2 * inner + offset2
            e = jnp.exp2(-jnp.abs(logits))
            u = 1.0 + e
            r = pl.reciprocal(u, approx=True)
            r = r * (2.0 - u * r)
            sig = jnp.where(logits >= 0.0, r, e * r)
            positive = iota((t_tile, wide), 0) == labels - (d * texts + at)
            grad = jnp.where(positive, sig - 1.0, sig)
            linear = jnp.maximum(jnp.where(positive, -logits, logits), 0.0)
            wt[pl.ds(at, t_tile), o * slots : o * slots + wide] = grad.astype(BF16)
            log_u = jnp.log(fold(u, lambda x, y: x * y))
            return (
                sums[0] + fold(linear, add),
                sums[1] + log_u + fold(e - (u - 1.0), add),
                sums[2] + fold(grad * inner, add),
                sums[3] + fold(grad, add),
            )

        sums = lax.fori_loop(0, texts // t_tile, chunk, (jnp.zeros((8, wide), F32),) * 4)
        for k in range(4):
            for g in range(n):
                sums_ref[k] += sums[k][:, g * slots : (g + 1) * slots]

    def image_terms(o, n):
        return mm_tn(wt[:, o * slots : (o + n) * slots], text_ref[...])

    n_text = text_half // t_tile
    mine = pl.ds(pl.multiple_of(s * text_half, text_half), text_half)
    theirs = pl.ds(pl.multiple_of((1 - s) * text_half, text_half), text_half)

    scores(0, 2, home[...])

    @pl.when(c == 1)
    def _():
        ext2_copy.start()

    own[...] = image_terms(0, 2)
    own_copy = remote(own, own_in, 4, partner)
    own_copy.start()
    text_sum[...] = mm(wt[theirs, : 2 * slots], home[...])
    gt[...] = mm(wt[mine, : 2 * slots], home[...])

    ext1_copy.wait_recv()
    ext1_fwd = remote(ext1(half_c), ext1(half_c), 5, partner)
    ext1_fwd.start()
    pre_copy = remote(pre.at[half_o], pre_in, 6, partner)
    ret1_copy = remote(ret1_out, ret1.at[half_c], 8, m_dev(1))
    ret2_copy = remote(ret2_out, ret2, 7, m_dev(2 * c - 1))
    text_copies = []
    for j in range(n_text):
        here = pl.ds(j * t_tile, t_tile)
        text_copies.append(remote(text_out.at[here], text_in.at[here], 15 + j, across))

    def send_text(o):
        for j in range(n_text):
            here = pl.ds(j * t_tile, t_tile)
            at = pl.ds(pl.multiple_of((1 - s) * text_half + j * t_tile, t_tile), t_tile)
            late = mm(wt[at, o * slots :], sl[(o - 2) * slots :, :])
            text_out[here, :] = (text_sum[here, :] + late).astype(BF16)
            text_copies[j].start()

    def send_pre():
        pre[...] = image_terms(2, 1)
        pre_copy.start()

    def send_ret1():
        pre_copy.wait_recv()
        ret1_out[...] = (pre[half_c, :] + pre_in[...]).astype(BF16)
        ret1_copy.start()

    def send_ret2():
        ret2_out[...] = image_terms(3, 1).astype(BF16)
        ret2_copy.start()

    @pl.when(c == 0)
    def _():
        ext2_copy.wait_recv()
        scores(3, 1, sl[slots:, :])
        ext1_fwd.wait_recv()
        scores(2, 1, sl[:slots, :])
        send_text(2)
        send_pre()
        send_ret1()
        send_ret2()

    @pl.when(c == 1)
    def _():
        ext1_fwd.wait_recv()
        scores(2, 1, sl[:slots, :])
        send_pre()
        text_sum[...] += mm(wt[theirs, 2 * slots : 3 * slots], sl[:slots, :])
        ext2_copy.wait_recv()
        scores(3, 1, sl[slots:, :])
        send_ret1()
        send_ret2()
        send_text(3)

    gt[...] += mm(wt[mine, 2 * slots :], sl[...])
    gt_copy = pltpu.make_async_copy(gt, gt_hbm, local_sem.at[5])
    gt_copy.start()

    lane = iota((8, LANES), 1)
    totals = [
        jnp.sum(x, keepdims=True)
        for x in (LN2 * sums_ref[0] + sums_ref[1], sums_ref[2], sums_ref[3])
    ]
    kind = lax.rem(lane, 3)
    stat[...] = jnp.where(kind == 0, totals[0], jnp.where(kind == 1, totals[1], totals[2]))
    stat_copy = remote(stat, stat_in, 9, partner)
    stat_copy.start()

    ret1_copy.wait_recv()
    ret1_fwd = remote(ret1.at[half_c], ret1.at[half_c], 13, partner)
    ret1_fwd.start()
    ret2_copy.wait_recv()
    ret2_fwd = remote(ret2, ret2b, 14, partner)
    ret2_fwd.start()
    own_copy.wait_recv()
    stat_copy.wait_recv()

    value = stat[...] + stat_in[...]
    top = value.astype(BF16).astype(F32)
    middle = (value - top).astype(BF16).astype(F32)
    low = value - top - middle
    payload = jnp.where(lane < 3, top, jnp.where(lane < 6, middle, jnp.where(lane < 9, low, 0.0)))

    ret1_fwd.wait_recv()
    odd = own[:slots, :] + own_in[:slots, :] + ret1[...].astype(F32)
    slot_grad[:slots, :] = (factor * odd).astype(BF16)
    ret2_fwd.wait_recv()
    evn = own[slots:, :] + own_in[slots:, :] + (ret2[...].astype(F32) + ret2b[...].astype(F32))
    slot_grad[slots:, :] = (factor * evn).astype(BF16)

    payload_rows = jnp.broadcast_to(payload[:per_chip][None], (row_tile // per_chip, per_chip, LANES))
    for r in range(rows // row_tile):
        n = row_tile // per_chip
        q_rows = q_t[r * row_tile : (r + 1) * row_tile, :]
        first = mm(q_rows, slot_grad[:, :width]).reshape(n, per_chip, width)
        second = mm(q_rows, slot_grad[:, width:]).reshape(n, per_chip, tail)
        second = jnp.concatenate([second, payload_rows], axis=2)
        back[r * n : (r + 1) * n] = jnp.concatenate([first, second], axis=1).astype(BF16)
        all_start(back, back_recv, 1, -1, r * n, (r + 1) * n)

    back_own = own_start(back, back_recv, 1)
    back_all = all_desc(back, back_recv, 1)
    for copy in text_copies:
        copy.wait_recv()
    p_copy.wait()
    gt_copy.wait()
    back_own.wait()
    back_all.wait_recv()

    out_all.wait_send()
    back_all.wait_send()
    for copy in (
        ext1_copy,
        ext2_copy,
        own_copy,
        ext1_fwd,
        pre_copy,
        ret2_copy,
        ret1_copy,
        stat_copy,
        ret1_fwd,
        ret2_fwd,
        *text_copies,
    ):
        copy.wait_send()


def finish(n_dp, pairs, per_chip, scale_ref, back_ref, text_in_ref, gt_in_ref, p_ref, *rest):
    gi_ref, gt_ref, loss_ref, gscale_ref, gbias_ref, rows_in = rest
    chips, _, width = back_ref.shape
    rows, columns = rows_in.shape
    tail = columns - width

    @pl.when(pl.program_id(0) == 0)
    def _():
        rows_in[:, :width] = (
            back_ref[:, :per_chip, :].astype(F32).reshape(rows, width).astype(BF16)
        )
        rows_in[:, width:] = (
            back_ref[:, per_chip:, :tail].astype(F32).reshape(rows, tail).astype(BF16)
        )
        chip = lax.div(lax.axis_index("dp"), 2) * 2 + lax.axis_index("sub")
        sums_in = back_ref[:, per_chip:, tail:].astype(F32)[:, 0, :].astype(BF16)
        source = (chip + (iota((chips, chips), 1) + 1) * STRIDE) & (chips - 1)
        order = (source == iota((chips, chips), 0)).astype(F32).astype(BF16)
        total = jnp.sum(mm(order, sums_in), axis=0, keepdims=True)
        lane = iota((1, LANES), 1)
        for k, ref in enumerate((loss_ref, gscale_ref, gbias_ref)):
            picked = (lane < 9) & (lax.rem(lane, 3) == k)
            ref[0] = jnp.sum(jnp.where(picked, total, 0.0)) / pairs

    gi_ref[...] = mm(p_ref[...], rows_in[...]).astype(BF16)
    gt_ref[...] = scale_ref[...] * (gt_in_ref[...] + text_in_ref[...].astype(F32))


def local(images, text_embeds, dest_slot, labels, logit_scale, logit_bias):
    n_dp = lax.axis_size("dp")
    rows, columns = images.shape
    texts = text_embeds.shape[0]
    slots = labels.shape[0]
    chips = n_dp
    per_chip = rows // chips
    width = (columns + LANES) // 2
    pairs = float(slots * n_dp * 2 * STOPS * texts)
    vmem = pl.BlockSpec(memory_space=pltpu.VMEM)
    smem = pl.BlockSpec(memory_space=pltpu.SMEM)
    hbm = pl.BlockSpec(memory_space=pl.ANY)
    message = pltpu.VMEM((chips, 2 * per_chip, width), BF16)

    def buf(n, dtype=BF16):
        return pltpu.VMEM((n, columns), dtype)

    scale = logit_scale.reshape(1, 1)
    back, text_in, gt, p_t = pl.pallas_call(
        functools.partial(kernel, n_dp),
        out_shape=(
            jax.ShapeDtypeStruct((chips, 2 * per_chip, width), BF16),
            jax.ShapeDtypeStruct((texts // 2, columns), BF16),
            jax.ShapeDtypeStruct((texts // 2, columns), F32),
            jax.ShapeDtypeStruct((rows, rows), BF16),
        ),
        in_specs=[vmem, vmem, vmem, vmem, vmem, hbm],
        out_specs=(hbm, hbm, hbm, hbm),
        scratch_shapes=[
            buf(texts),
            message,
            message,
            message,
            buf(2 * slots),
            buf(2 * slots),
            buf(2 * slots),
            buf(2 * slots),
            pltpu.VMEM((4, 1, slots), jnp.int32),
            pltpu.VMEM((texts, 4 * slots), BF16),
            pltpu.VMEM((texts, 2 * slots), F32),
            pltpu.VMEM((4, 8, slots), F32),
            buf(2 * slots, F32),
            buf(2 * slots, F32),
            buf(slots, F32),
            buf(slots // 2, F32),
            buf(slots // 2),
            buf(slots),
            buf(slots),
            buf(slots),
            buf(slots),
            buf(2 * slots),
            buf(texts // 2, F32),
            buf(texts // 2),
            buf(texts // 2, F32),
            pltpu.VMEM((rows, rows), BF16),
            pltpu.VMEM((rows, 2 * slots), BF16),
            pltpu.VMEM((8, LANES), F32),
            pltpu.VMEM((8, LANES), F32),
            pltpu.SemaphoreType.DMA((2,)),
            pltpu.SemaphoreType.DMA((2,)),
            pltpu.SemaphoreType.DMA((6,)),
            pltpu.SemaphoreType.DMA((24,)),
            pltpu.SemaphoreType.DMA((24,)),
        ],
        compiler_params=pltpu.CompilerParams(
            collective_id=0,
            has_side_effects=True,
            vmem_limit_bytes=58 * 1024 * 1024,
        ),
    )(
        scale,
        logit_bias.reshape(1, 1),
        dest_slot.reshape(1, rows),
        labels.reshape(1, slots),
        images,
        text_embeds,
    )
    tiles = 4
    tile_rows = pl.BlockSpec((rows // tiles, columns), lambda i: (i, 0))
    tile_texts = pl.BlockSpec((texts // 2 // tiles, columns), lambda i: (i, 0))
    scalar = jax.ShapeDtypeStruct((1,), F32)
    return pl.pallas_call(
        functools.partial(finish, n_dp, pairs, per_chip),
        out_shape=(
            jax.ShapeDtypeStruct((rows, columns), BF16),
            jax.ShapeDtypeStruct((texts // 2, columns), F32),
            scalar,
            scalar,
            scalar,
        ),
        grid=(tiles,),
        in_specs=[
            pl.BlockSpec((1, 1), lambda i: (0, 0)),
            pl.BlockSpec(back.shape, lambda i: (0, 0, 0)),
            tile_texts,
            tile_texts,
            pl.BlockSpec((rows // tiles, rows), lambda i: (i, 0)),
        ],
        out_specs=(tile_rows, tile_texts, smem, smem, smem),
        scratch_shapes=[buf(rows)],
        compiler_params=pltpu.CompilerParams(vmem_limit_bytes=60 * 1024 * 1024),
    )(scale, back, text_in, gt, p_t)


def solution(mesh):
    return jax.shard_map(
        local,
        mesh=mesh,
        in_specs=(
            P(("dp", "sub"), None),
            P("dp", None),
            P(("dp", "sub")),
            P(("dp", "sub")),
            P(),
            P(),
        ),
        out_specs=(P(("dp", "sub"), None), P(("dp", "sub"), None), P(), P(), P()),
        check_vma=False,
    )
```

```python
import functools

import jax
import jax.numpy as jnp
from jax import lax
from jax.experimental import pallas as pl
from jax.experimental.pallas import tpu as pltpu
from jax.sharding import PartitionSpec as P

STOPS = 4
LANES = 128
MESH = pl.DeviceIdType.MESH
STRIDE, UNSTRIDE = 27, 19
LOG2E = 1.4426950408889634
LN2 = 0.6931471805599453
F32 = jnp.float32
BF16 = jnp.bfloat16


def iota(shape, axis):
    return lax.broadcasted_iota(jnp.int32, shape, axis)


def mm(a, b):
    return lax.dot_general(a, b, (((1,), (0,)), ((), ())), preferred_element_type=F32)


def mm_tn(a, b):
    return lax.dot_general(a, b, (((0,), (0,)), ((), ())), preferred_element_type=F32)


def fold(x, op):
    while x.shape[0] > 8:
        n = x.shape[0] // 2
        x = op(x[:n], x[n:])
    return x


def mm_nt(a, b):
    return lax.dot_general(a, b, (((1,), (1,)), ((), ())), preferred_element_type=F32)


def kernel(
    n_dp,
    scale_ref,
    bias_ref,
    dest_ref,
    labels_ref,
    images_ref,
    text_hbm,
    back_recv,
    text_in,
    gt_hbm,
    p_hbm,
    text_ref,
    send,
    recv,
    back,
    home,
    part,
    part_in,
    sl,
    lab,
    wt,
    inner_ref,
    sums_ref,
    own,
    own_in,
    pre,
    pre_in,
    ret1_out,
    ret1,
    ret2_out,
    ret2,
    ret2b,
    slot_grad,
    text_sum,
    text_out,
    gt,
    p_t,
    q_t,
    stat,
    stat_in,
    a2a_send,
    a2a_recv,
    local_sem,
    ss,
    rs,
):
    rows, columns = images_ref.shape
    texts = text_ref.shape[0]
    text_half = texts // 2
    slots = labels_ref.shape[1]
    half = slots // 2
    chips = n_dp
    n_m = n_dp // 2
    per_chip = rows // chips
    width = send.shape[2]
    tail = columns - width
    t_tile = min(256, texts // 2)

    d = lax.axis_index("dp")
    s = lax.axis_index("sub")
    m = lax.div(d, 2)
    c = lax.rem(d, 2)
    chip = m * 2 + s
    upper = lax.div(m, n_m // 2)
    half_here = lax.rem(s + upper, 2)
    partner = (m * 2 + (1 - c), s)
    across = (d, 1 - s)

    def chip_dev(i):
        i = lax.rem(i + chips, chips)
        return (lax.div(i, 2) * 2 + c, lax.rem(i, 2))

    def m_dev(step):
        there = lax.rem(m + step + n_m, n_m)
        return (there * 2 + c, lax.rem(half_here + lax.div(there, n_m // 2), 2))

    def labels_to(step):
        there = lax.rem(d - step + n_dp, n_dp)
        return (there, lax.rem(s + lax.div(there, n_dp // 2), 2))

    def labels_from(step):
        return (lax.rem(d + step, n_dp), half_here)

    text_copy = pltpu.make_async_copy(text_hbm, text_ref, local_sem.at[3])
    text_copy.start()

    barrier = pltpu.get_barrier_semaphore()

    def greet(k, carry):
        pl.semaphore_signal(barrier, inc=1, device_id=chip_dev(chip + k), device_id_type=MESH)
        return carry

    lax.fori_loop(1, chips, greet, 0)
    for dev in (partner, labels_from(1), labels_from(3)):
        pl.semaphore_signal(barrier, inc=1, device_id=dev, device_id_type=MESH)

    def remote(src, dst, k, dev):
        return pltpu.make_async_remote_copy(
            src_ref=src,
            dst_ref=dst,
            send_sem=ss.at[k],
            recv_sem=rs.at[k],
            device_id=dev,
            device_id_type=MESH,
        )

    q = dest_ref[...]
    valid = q >= 0
    group = lax.div(jnp.maximum(q, 0), 2 * slots)
    rest = jnp.maximum(q, 0) - group * (2 * slots)
    to_sub = lax.div(rest, slots)
    slot_id = rest - to_sub * slots
    even = (group & 1) == 0
    to_m = lax.div((group + (n_dp - 1)) & (n_dp - 1), 2)
    to_sub = (to_sub + lax.div(to_m, n_m // 2)) & 1
    rel = ((to_m * 2 + to_sub - chip + chips) * UNSTRIDE + (chips - 1)) & (chips - 1)
    rel = jnp.where(valid, rel, -1)
    onehot = rel == iota((chips, rows), 0)
    earlier = (iota((rows, rows), 0) < iota((rows, rows), 1)).astype(F32).astype(BF16)
    onehot_f = onehot.astype(F32)
    rank = mm(onehot_f.astype(BF16), earlier)
    within = jnp.sum(onehot_f * rank, axis=0, keepdims=True)
    placed = jnp.where(valid, rel.astype(F32) * float(per_chip) + within, -1.0)
    placed_col = jnp.transpose(jnp.broadcast_to(placed, (LANES, rows)))[:, :1].astype(jnp.int32)
    p_t[...] = (placed_col == iota((rows, rows), 1)).astype(F32).astype(BF16)
    p_copy = pltpu.make_async_copy(p_t, p_hbm, local_sem.at[4])
    p_copy.start()
    placed_int = placed.astype(jnp.int32)
    id_plus = (slot_id + 1).astype(F32)
    id_odd = jnp.where(valid & jnp.logical_not(even), id_plus, 0.0)
    id_even = jnp.where(valid & even, id_plus, 0.0)
    which = iota((LANES, rows), 0)
    id_rows = jnp.where(which == 0, id_odd, jnp.where(which == 1, id_even, 0.0))
    ids_block = jnp.transpose(id_rows).astype(BF16)
    row_tile = min(128, rows)
    for r in range(rows // row_tile):
        p_mat = (placed_int == iota((row_tile, rows), 0) + r * row_tile).astype(F32).astype(BF16)
        n = row_tile // per_chip
        first = mm(p_mat, images_ref[:, :width]).reshape(n, per_chip, width)
        second = mm(p_mat, images_ref[:, width:]).reshape(n, per_chip, tail)
        third = mm(p_mat, ids_block).reshape(n, per_chip, LANES)
        second = jnp.concatenate([second, third], axis=2)
        send[r * n : (r + 1) * n] = jnp.concatenate([first, second], axis=1).astype(BF16)

    pl.semaphore_wait(barrier, chips - 1 + 3)

    lab_copies = [
        remote(labels_ref, lab.at[slot], 9 + step, labels_to(step))
        for step, slot in ((1, 1 - c), (2, 1 + c), (3, 3 - c))
    ]
    for copy in lab_copies:
        copy.start()
    lab_own = pltpu.make_async_copy(labels_ref, lab.at[3 - 3 * c], local_sem.at[0])
    lab_swap = remote(labels_ref, lab.at[3 - 3 * c], 20, across)

    @pl.when(upper == 0)
    def _():
        lab_own.start()

    @pl.when(upper == 1)
    def _():
        lab_swap.start()


    def all_start(buf, into, which_sem, sign, lo, hi):
        def step(k, carry):
            pltpu.make_async_remote_copy(
                src_ref=buf.at[k],
                dst_ref=into.at[k],
                send_sem=a2a_send.at[which_sem],
                recv_sem=a2a_recv.at[which_sem],
                device_id=chip_dev(chip + sign * lax.rem((k + 1) * STRIDE, chips)),
                device_id_type=MESH,
            ).start()
            return carry

        lax.fori_loop(lo, min(hi, chips - 1), step, 0)

    def own_start(buf, into, which_sem):
        copy = pltpu.make_async_copy(
            buf.at[chips - 1], into.at[chips - 1], local_sem.at[1 + which_sem]
        )
        copy.start()
        return copy

    def all_desc(buf, into, which_sem):
        return pltpu.make_async_remote_copy(
            src_ref=buf.at[pl.ds(0, chips - 1)],
            dst_ref=into.at[pl.ds(0, chips - 1)],
            send_sem=a2a_send.at[which_sem],
            recv_sem=a2a_recv.at[which_sem],
            device_id=partner,
            device_id_type=MESH,
        )

    all_start(send, recv, 0, 1, 0, chips)
    out_own = own_start(send, recv, 0)
    out_all = all_desc(send, recv, 0)
    out_own.wait()
    out_all.wait_recv()

    ids = recv[:, per_chip:, tail:].astype(F32).reshape(rows, LANES).astype(jnp.int32)
    lane = iota((rows, 2 * slots), 1)
    filled = jnp.where(lane < slots, ids[:, :1], ids[:, 1:2] + slots)
    q_t[...] = (filled == lane + 1).astype(F32).astype(BF16)
    ids_t = jnp.transpose(ids.astype(F32)).astype(jnp.int32)
    first = recv[:, :per_chip, :].astype(F32).reshape(rows, width).astype(BF16)
    second = recv[:, per_chip:, :tail].astype(F32).reshape(rows, tail).astype(BF16)
    part_copies = []
    for g in range(2):
        q_mat = (ids_t[g : g + 1, :] == iota((slots, rows), 0) + 1).astype(F32).astype(BF16)
        here = pl.ds(g * slots, slots)
        part[here, :width] = mm(q_mat, first).astype(BF16)
        part[here, width:] = mm(q_mat, second).astype(BF16)
        copy = remote(part.at[here], part_in.at[here], g, partner)
        copy.start()
        part_copies.append(copy)

    @pl.when(upper == 0)
    def _():
        lab_own.wait()

    @pl.when(upper == 1)
    def _():
        lab_swap.wait()

    for copy in lab_copies:
        copy.wait()
    for g in range(2):
        part_copies[g].wait()
        here = pl.ds(g * slots, slots)
        home[here, :] = (part[here, :].astype(F32) + part_in[here, :].astype(F32)).astype(BF16)
    half_c = pl.ds(pl.multiple_of(c * half, half), half)
    half_o = pl.ds(pl.multiple_of((1 - c) * half, half), half)

    def ext1(which_half):
        return sl.at[which_half]

    ext1_copy = remote(home.at[half_c], ext1(half_c), 2, m_dev(-1))
    ext1_copy.start()
    ext2_copy = remote(home.at[pl.ds(slots, slots)], sl.at[pl.ds(slots, slots)], 3, m_dev(1 - 2 * c))

    @pl.when(c == 0)
    def _():
        ext2_copy.start()

    text_copy.wait()

    factor = scale_ref[...]
    factor2 = factor * LOG2E
    offset2 = bias_ref[...] * LOG2E
    sums_ref[...] = jnp.zeros_like(sums_ref)

    def add(x, y):
        return x + y

    def scores(o, n, slot_rows):
        wide = n * slots
        inner_ref[:, :wide] = mm_nt(text_ref[...], slot_rows)
        labels = lab[o] if n == 1 else jnp.concatenate([lab[o], lab[o + 1]], axis=1)

        def chunk(j, sums):
            at = pl.multiple_of(j * t_tile, t_tile)
            inner = inner_ref[pl.ds(at, t_tile), :wide]
            logits = factor2 * inner + offset2
            e = jnp.exp2(-jnp.abs(logits))
            u = 1.0 + e
            r = pl.reciprocal(u, approx=True)
            r = r * (2.0 - u * r)
            sig = jnp.where(logits >= 0.0, r, e * r)
            positive = iota((t_tile, wide), 0) == labels - (d * texts + at)
            grad = jnp.where(positive, sig - 1.0, sig)
            linear = jnp.maximum(jnp.where(positive, -logits, logits), 0.0)
            wt[pl.ds(at, t_tile), o * slots : o * slots + wide] = grad.astype(BF16)
            log_u = jnp.log(fold(u, lambda x, y: x * y))
            return (
                sums[0] + fold(linear, add),
                sums[1] + log_u + fold(e - (u - 1.0), add),
                sums[2] + fold(grad * inner, add),
                sums[3] + fold(grad, add),
            )

        sums = lax.fori_loop(0, texts // t_tile, chunk, (jnp.zeros((8, wide), F32),) * 4)
        for k in range(4):
            for g in range(n):
                sums_ref[k] += sums[k][:, g * slots : (g + 1) * slots]

    def image_terms(o, n):
        return mm_tn(wt[:, o * slots : (o + n) * slots], text_ref[...])

    n_text = text_half // t_tile
    mine = pl.ds(pl.multiple_of(s * text_half, text_half), text_half)
    theirs = pl.ds(pl.multiple_of((1 - s) * text_half, text_half), text_half)

    scores(0, 2, home[...])

    @pl.when(c == 1)
    def _():
        ext2_copy.start()

    own[...] = image_terms(0, 2)
    own_copy = remote(own, own_in, 4, partner)
    own_copy.start()
    text_sum[...] = mm(wt[theirs, : 2 * slots], home[...])
    gt[...] = mm(wt[mine, : 2 * slots], home[...])

    ext1_copy.wait_recv()
    ext1_fwd = remote(ext1(half_c), ext1(half_c), 5, partner)
    ext1_fwd.start()
    pre_copy = remote(pre.at[half_o], pre_in, 6, partner)
    ret1_copy = remote(ret1_out, ret1.at[half_c], 8, m_dev(1))
    ret2_copy = remote(ret2_out, ret2, 7, m_dev(2 * c - 1))
    text_copies = []
    for j in range(n_text):
        here = pl.ds(j * t_tile, t_tile)
        text_copies.append(remote(text_out.at[here], text_in.at[here], 15 + j, across))

    def send_text(o):
        for j in range(n_text):
            here = pl.ds(j * t_tile, t_tile)
            at = pl.ds(pl.multiple_of((1 - s) * text_half + j * t_tile, t_tile), t_tile)
            late = mm(wt[at, o * slots :], sl[(o - 2) * slots :, :])
            text_out[here, :] = (text_sum[here, :] + late).astype(BF16)
            text_copies[j].start()

    def send_pre():
        pre[...] = image_terms(2, 1)
        pre_copy.start()

    def send_ret1():
        pre_copy.wait_recv()
        ret1_out[...] = (pre[half_c, :] + pre_in[...]).astype(BF16)
        ret1_copy.start()

    def send_ret2():
        ret2_out[...] = image_terms(3, 1).astype(BF16)
        ret2_copy.start()

    @pl.when(c == 0)
    def _():
        ext2_copy.wait_recv()
        scores(3, 1, sl[slots:, :])
        ext1_fwd.wait_recv()
        scores(2, 1, sl[:slots, :])
        send_text(2)
        send_pre()
        send_ret1()
        send_ret2()

    @pl.when(c == 1)
    def _():
        ext1_fwd.wait_recv()
        scores(2, 1, sl[:slots, :])
        send_pre()
        text_sum[...] += mm(wt[theirs, 2 * slots : 3 * slots], sl[:slots, :])
        ext2_copy.wait_recv()
        scores(3, 1, sl[slots:, :])
        send_ret1()
        send_ret2()
        send_text(3)

    gt[...] += mm(wt[mine, 2 * slots :], sl[...])
    gt_copy = pltpu.make_async_copy(gt, gt_hbm, local_sem.at[5])
    gt_copy.start()

    lane = iota((8, LANES), 1)
    totals = [
        jnp.sum(x, keepdims=True)
        for x in (LN2 * sums_ref[0] + sums_ref[1], sums_ref[2], sums_ref[3])
    ]
    kind = lax.rem(lane, 3)
    stat[...] = jnp.where(kind == 0, totals[0], jnp.where(kind == 1, totals[1], totals[2]))
    stat_copy = remote(stat, stat_in, 9, partner)
    stat_copy.start()

    ret1_copy.wait_recv()
    ret1_fwd = remote(ret1.at[half_c], ret1.at[half_c], 13, partner)
    ret1_fwd.start()
    ret2_copy.wait_recv()
    ret2_fwd = remote(ret2, ret2b, 14, partner)
    ret2_fwd.start()
    own_copy.wait_recv()
    stat_copy.wait_recv()

    value = stat[...] + stat_in[...]
    top = value.astype(BF16).astype(F32)
    middle = (value - top).astype(BF16).astype(F32)
    low = value - top - middle
    payload = jnp.where(lane < 3, top, jnp.where(lane < 6, middle, jnp.where(lane < 9, low, 0.0)))

    ret1_fwd.wait_recv()
    odd = own[:slots, :] + own_in[:slots, :] + ret1[...].astype(F32)
    slot_grad[:slots, :] = (factor * odd).astype(BF16)
    ret2_fwd.wait_recv()
    evn = own[slots:, :] + own_in[slots:, :] + (ret2[...].astype(F32) + ret2b[...].astype(F32))
    slot_grad[slots:, :] = (factor * evn).astype(BF16)

    payload_rows = jnp.broadcast_to(payload[:per_chip][None], (row_tile // per_chip, per_chip, LANES))
    for r in range(rows // row_tile):
        n = row_tile // per_chip
        q_rows = q_t[r * row_tile : (r + 1) * row_tile, :]
        first = mm(q_rows, slot_grad[:, :width]).reshape(n, per_chip, width)
        second = mm(q_rows, slot_grad[:, width:]).reshape(n, per_chip, tail)
        second = jnp.concatenate([second, payload_rows], axis=2)
        back[r * n : (r + 1) * n] = jnp.concatenate([first, second], axis=1).astype(BF16)
        all_start(back, back_recv, 1, -1, r * n, (r + 1) * n)

    back_own = own_start(back, back_recv, 1)
    back_all = all_desc(back, back_recv, 1)
    for copy in text_copies:
        copy.wait_recv()
    p_copy.wait()
    gt_copy.wait()
    back_own.wait()
    back_all.wait_recv()

    out_all.wait_send()
    back_all.wait_send()
    for copy in (
        ext1_copy,
        ext2_copy,
        own_copy,
        ext1_fwd,
        pre_copy,
        ret2_copy,
        ret1_copy,
        stat_copy,
        ret1_fwd,
        ret2_fwd,
        *text_copies,
    ):
        copy.wait_send()


def finish(n_dp, pairs, per_chip, scale_ref, back_ref, text_in_ref, gt_in_ref, p_ref, *rest):
    gi_ref, gt_ref, loss_ref, gscale_ref, gbias_ref, rows_in = rest
    chips, _, width = back_ref.shape
    rows, columns = rows_in.shape
    tail = columns - width

    @pl.when(pl.program_id(0) == 0)
    def _():
        rows_in[:, :width] = (
            back_ref[:, :per_chip, :].astype(F32).reshape(rows, width).astype(BF16)
        )
        rows_in[:, width:] = (
            back_ref[:, per_chip:, :tail].astype(F32).reshape(rows, tail).astype(BF16)
        )
        chip = lax.div(lax.axis_index("dp"), 2) * 2 + lax.axis_index("sub")
        sums_in = back_ref[:, per_chip:, tail:].astype(F32)[:, 0, :].astype(BF16)
        source = (chip + (iota((chips, chips), 1) + 1) * STRIDE) & (chips - 1)
        order = (source == iota((chips, chips), 0)).astype(F32).astype(BF16)
        total = jnp.sum(mm(order, sums_in), axis=0, keepdims=True)
        lane = iota((1, LANES), 1)
        for k, ref in enumerate((loss_ref, gscale_ref, gbias_ref)):
            picked = (lane < 9) & (lax.rem(lane, 3) == k)
            ref[0] = jnp.sum(jnp.where(picked, total, 0.0)) / pairs

    gi_ref[...] = mm(p_ref[...], rows_in[...]).astype(BF16)
    gt_ref[...] = scale_ref[...] * (gt_in_ref[...] + text_in_ref[...].astype(F32))


def local(images, text_embeds, dest_slot, labels, logit_scale, logit_bias):
    n_dp = lax.axis_size("dp")
    rows, columns = images.shape
    texts = text_embeds.shape[0]
    slots = labels.shape[0]
    chips = n_dp
    per_chip = rows // chips
    width = (columns + LANES) // 2
    pairs = float(slots * n_dp * 2 * STOPS * texts)
    vmem = pl.BlockSpec(memory_space=pltpu.VMEM)
    smem = pl.BlockSpec(memory_space=pltpu.SMEM)
    hbm = pl.BlockSpec(memory_space=pl.ANY)
    message = pltpu.VMEM((chips, 2 * per_chip, width), BF16)

    def buf(n, dtype=BF16):
        return pltpu.VMEM((n, columns), dtype)

    scale = logit_scale.reshape(1, 1)
    back, text_in, gt, p_t = pl.pallas_call(
        functools.partial(kernel, n_dp),
        out_shape=(
            jax.ShapeDtypeStruct((chips, 2 * per_chip, width), BF16),
            jax.ShapeDtypeStruct((texts // 2, columns), BF16),
            jax.ShapeDtypeStruct((texts // 2, columns), F32),
            jax.ShapeDtypeStruct((rows, rows), BF16),
        ),
        in_specs=[vmem, vmem, vmem, vmem, vmem, hbm],
        out_specs=(hbm, hbm, hbm, hbm),
        scratch_shapes=[
            buf(texts),
            message,
            message,
            message,
            buf(2 * slots),
            buf(2 * slots),
            buf(2 * slots),
            buf(2 * slots),
            pltpu.VMEM((4, 1, slots), jnp.int32),
            pltpu.VMEM((texts, 4 * slots), BF16),
            pltpu.VMEM((texts, 2 * slots), F32),
            pltpu.VMEM((4, 8, slots), F32),
            buf(2 * slots, F32),
            buf(2 * slots, F32),
            buf(slots, F32),
            buf(slots // 2, F32),
            buf(slots // 2),
            buf(slots),
            buf(slots),
            buf(slots),
            buf(slots),
            buf(2 * slots),
            buf(texts // 2, F32),
            buf(texts // 2),
            buf(texts // 2, F32),
            pltpu.VMEM((rows, rows), BF16),
            pltpu.VMEM((rows, 2 * slots), BF16),
            pltpu.VMEM((8, LANES), F32),
            pltpu.VMEM((8, LANES), F32),
            pltpu.SemaphoreType.DMA((2,)),
            pltpu.SemaphoreType.DMA((2,)),
            pltpu.SemaphoreType.DMA((6,)),
            pltpu.SemaphoreType.DMA((24,)),
            pltpu.SemaphoreType.DMA((24,)),
        ],
        compiler_params=pltpu.CompilerParams(
            collective_id=0,
            has_side_effects=True,
            vmem_limit_bytes=58 * 1024 * 1024,
        ),
    )(
        scale,
        logit_bias.reshape(1, 1),
        dest_slot.reshape(1, rows),
        labels.reshape(1, slots),
        images,
        text_embeds,
    )
    tiles = 2
    tile_rows = pl.BlockSpec((rows // tiles, columns), lambda i: (i, 0))
    tile_texts = pl.BlockSpec((texts // 2 // tiles, columns), lambda i: (i, 0))
    scalar = jax.ShapeDtypeStruct((1,), F32)
    return pl.pallas_call(
        functools.partial(finish, n_dp, pairs, per_chip),
        out_shape=(
            jax.ShapeDtypeStruct((rows, columns), BF16),
            jax.ShapeDtypeStruct((texts // 2, columns), F32),
            scalar,
            scalar,
            scalar,
        ),
        grid=(tiles,),
        in_specs=[
            pl.BlockSpec((1, 1), lambda i: (0, 0)),
            pl.BlockSpec(back.shape, lambda i: (0, 0, 0)),
            tile_texts,
            tile_texts,
            pl.BlockSpec((rows // tiles, rows), lambda i: (i, 0)),
        ],
        out_specs=(tile_rows, tile_texts, smem, smem, smem),
        scratch_shapes=[buf(rows)],
        compiler_params=pltpu.CompilerParams(vmem_limit_bytes=60 * 1024 * 1024),
    )(scale, back, text_in, gt, p_t)


def solution(mesh):
    return jax.shard_map(
        local,
        mesh=mesh,
        in_specs=(
            P(("dp", "sub"), None),
            P("dp", None),
            P(("dp", "sub")),
            P(("dp", "sub")),
            P(),
            P(),
        ),
        out_specs=(P(("dp", "sub"), None), P(("dp", "sub"), None), P(), P(), P()),
        check_vma=False,
    )
```

```python
import functools

import jax
import jax.numpy as jnp
from jax import lax
from jax.experimental import pallas as pl
from jax.experimental.pallas import tpu as pltpu
from jax.sharding import PartitionSpec as P

STOPS = 4
LANES = 128
MESH = pl.DeviceIdType.MESH
STRIDE, UNSTRIDE = 27, 19
LOG2E = 1.4426950408889634
LN2 = 0.6931471805599453
F32 = jnp.float32
BF16 = jnp.bfloat16


def iota(shape, axis):
    return lax.broadcasted_iota(jnp.int32, shape, axis)


def mm(a, b):
    return lax.dot_general(a, b, (((1,), (0,)), ((), ())), preferred_element_type=F32)


def mm_tn(a, b):
    return lax.dot_general(a, b, (((0,), (0,)), ((), ())), preferred_element_type=F32)


def fold(x, op):
    while x.shape[0] > 8:
        n = x.shape[0] // 2
        x = op(x[:n], x[n:])
    return x


def mm_nt(a, b):
    return lax.dot_general(a, b, (((1,), (1,)), ((), ())), preferred_element_type=F32)


def kernel(
    n_dp,
    scale_ref,
    bias_ref,
    dest_ref,
    labels_ref,
    images_ref,
    text_hbm,
    back_in,
    stats_in,
    text_in,
    gt_hbm,
    placed_hbm,
    text_ref,
    send,
    recv,
    back,
    home,
    part,
    part_in,
    sl,
    lab,
    wt,
    inner_ref,
    sums_ref,
    own,
    own_in,
    pre,
    pre_in,
    ret1_out,
    ret1,
    ret2_out,
    ret2,
    ret2b,
    grad_rows,
    text_sum,
    text_out,
    gt,
    placed_ref,
    q_t,
    stat,
    stat_in,
    a2a_send,
    a2a_recv,
    local_sem,
    ss,
    rs,
):
    rows, columns = images_ref.shape
    texts = text_ref.shape[0]
    text_half = texts // 2
    slots = labels_ref.shape[1]
    half = slots // 2
    chips = n_dp
    n_m = n_dp // 2
    per_chip = rows // chips
    width = send.shape[2]
    tail = columns - width
    t_tile = min(256, texts // 2)

    d = lax.axis_index("dp")
    s = lax.axis_index("sub")
    m = lax.div(d, 2)
    c = lax.rem(d, 2)
    chip = m * 2 + s
    upper = lax.div(m, n_m // 2)
    half_here = lax.rem(s + upper, 2)
    partner = (m * 2 + (1 - c), s)
    across = (d, 1 - s)

    def chip_dev(i):
        i = lax.rem(i + chips, chips)
        return (lax.div(i, 2) * 2 + c, lax.rem(i, 2))

    def m_dev(step):
        there = lax.rem(m + step + n_m, n_m)
        return (there * 2 + c, lax.rem(half_here + lax.div(there, n_m // 2), 2))

    def labels_to(step):
        there = lax.rem(d - step + n_dp, n_dp)
        return (there, lax.rem(s + lax.div(there, n_dp // 2), 2))

    def labels_from(step):
        return (lax.rem(d + step, n_dp), half_here)

    text_copy = pltpu.make_async_copy(text_hbm, text_ref, local_sem.at[7])
    text_copy.start()

    barrier = pltpu.get_barrier_semaphore()

    def greet(k, carry):
        pl.semaphore_signal(barrier, inc=1, device_id=chip_dev(chip + k), device_id_type=MESH)
        return carry

    lax.fori_loop(1, chips, greet, 0)
    for dev in (partner, labels_from(1), labels_from(3)):
        pl.semaphore_signal(barrier, inc=1, device_id=dev, device_id_type=MESH)

    def remote(src, dst, k, dev):
        return pltpu.make_async_remote_copy(
            src_ref=src,
            dst_ref=dst,
            send_sem=ss.at[k],
            recv_sem=rs.at[k],
            device_id=dev,
            device_id_type=MESH,
        )

    q = dest_ref[...]
    valid = q >= 0
    group = lax.div(jnp.maximum(q, 0), 2 * slots)
    rest = jnp.maximum(q, 0) - group * (2 * slots)
    to_sub = lax.div(rest, slots)
    slot_id = rest - to_sub * slots
    even = (group & 1) == 0
    to_m = lax.div((group + (n_dp - 1)) & (n_dp - 1), 2)
    to_sub = (to_sub + lax.div(to_m, n_m // 2)) & 1
    rel = ((to_m * 2 + to_sub - chip + chips) * UNSTRIDE + (chips - 1)) & (chips - 1)
    rel = jnp.where(valid, rel, -1)
    onehot = rel == iota((chips, rows), 0)
    earlier = (iota((rows, rows), 0) < iota((rows, rows), 1)).astype(F32).astype(BF16)
    onehot_f = onehot.astype(F32)
    rank = mm(onehot_f.astype(BF16), earlier)
    within = jnp.sum(onehot_f * rank, axis=0, keepdims=True)
    placed = jnp.where(valid, rel.astype(F32) * float(per_chip) + within, -1.0)
    placed_int = placed.astype(jnp.int32)
    placed_ref[...] = placed_int
    placed_copy = pltpu.make_async_copy(placed_ref, placed_hbm, local_sem.at[4])
    placed_copy.start()
    id_plus = (slot_id + 1).astype(F32)
    id_odd = jnp.where(valid & jnp.logical_not(even), id_plus, 0.0)
    id_even = jnp.where(valid & even, id_plus, 0.0)
    which = iota((LANES, rows), 0)
    id_rows = jnp.where(which == 0, id_odd, jnp.where(which == 1, id_even, 0.0))
    ids_block = jnp.transpose(id_rows).astype(BF16)
    row_tile = min(128, rows)
    for r in range(rows // row_tile):
        p_mat = (placed_int == iota((row_tile, rows), 0) + r * row_tile).astype(F32).astype(BF16)
        n = row_tile // per_chip
        first = mm(p_mat, images_ref[:, :width]).reshape(n, per_chip, width)
        second = mm(p_mat, images_ref[:, width:]).reshape(n, per_chip, tail)
        third = mm(p_mat, ids_block).reshape(n, per_chip, LANES)
        second = jnp.concatenate([second, third], axis=2)
        send[r * n : (r + 1) * n] = jnp.concatenate([first, second], axis=1).astype(BF16)

    pl.semaphore_wait(barrier, chips - 1 + 3)

    lab_copies = [
        remote(labels_ref, lab.at[slot], 9 + step, labels_to(step))
        for step, slot in ((1, 1 - c), (2, 1 + c), (3, 3 - c))
    ]
    for copy in lab_copies:
        copy.start()
    lab_own = pltpu.make_async_copy(labels_ref, lab.at[3 - 3 * c], local_sem.at[6])
    lab_swap = remote(labels_ref, lab.at[3 - 3 * c], 20, across)

    @pl.when(upper == 0)
    def _():
        lab_own.start()

    @pl.when(upper == 1)
    def _():
        lab_swap.start()


    def all_start(src, dst, own_src, own_dst, total, which_sem, sign):
        def step(k, carry):
            to = lax.rem(chip + sign * lax.rem((k + 1) * STRIDE, chips) + chips, chips)
            swaps = lax.rem(to, 2) + s + lax.div(to, chips // 2) + upper

            @pl.when(lax.rem(swaps, 2) == carry)
            def _():
                pltpu.make_async_remote_copy(
                    src_ref=src(k),
                    dst_ref=dst(k),
                    send_sem=a2a_send.at[which_sem],
                    recv_sem=a2a_recv.at[which_sem],
                    device_id=chip_dev(to),
                    device_id_type=MESH,
                ).start()

            return carry

        def step_any(k, carry):
            pltpu.make_async_remote_copy(
                src_ref=src(k),
                dst_ref=dst(k),
                send_sem=a2a_send.at[which_sem],
                recv_sem=a2a_recv.at[which_sem],
                device_id=chip_dev(chip + sign * lax.rem((k + 1) * STRIDE, chips)),
                device_id_type=MESH,
            ).start()
            return carry

        if which_sem == 0:
            lax.fori_loop(0, chips - 1, step_any, 0)
        else:
            for turn in range(2):
                lax.fori_loop(0, chips - 1, step, turn)
        own_copy = pltpu.make_async_copy(own_src, own_dst, local_sem.at[which_sem])
        own_copy.start()
        all_copy = pltpu.make_async_remote_copy(
            src_ref=total.at[pl.ds(0, chips - 1)],
            dst_ref=total.at[pl.ds(0, chips - 1)],
            send_sem=a2a_send.at[which_sem],
            recv_sem=a2a_recv.at[which_sem],
            device_id=partner,
            device_id_type=MESH,
        )
        return own_copy, all_copy

    last = chips - 1
    out_own, out_all = all_start(
        lambda k: send.at[k], lambda k: recv.at[k], send.at[last], recv.at[last], recv, 0, 1
    )
    out_own.wait()
    out_all.wait_recv()

    ids = recv[:, per_chip:, tail:].astype(F32).reshape(rows, LANES).astype(jnp.int32)
    lane = iota((rows, 2 * slots), 1)
    filled = jnp.where(lane < slots, ids[:, :1], ids[:, 1:2] + slots)
    q_t[...] = (filled == lane + 1).astype(F32).astype(BF16)
    ids_t = jnp.transpose(ids.astype(F32)).astype(jnp.int32)
    first = recv[:, :per_chip, :].astype(F32).reshape(rows, width).astype(BF16)
    second = recv[:, per_chip:, :tail].astype(F32).reshape(rows, tail).astype(BF16)
    part_copies = []
    for g in range(2):
        q_mat = (ids_t[g : g + 1, :] == iota((slots, rows), 0) + 1).astype(F32).astype(BF16)
        here = pl.ds(g * slots, slots)
        part[here, :width] = mm(q_mat, first).astype(BF16)
        part[here, width:] = mm(q_mat, second).astype(BF16)
        copy = remote(part.at[here], part_in.at[here], g, partner)
        copy.start()
        part_copies.append(copy)

    @pl.when(upper == 0)
    def _():
        lab_own.wait()

    @pl.when(upper == 1)
    def _():
        lab_swap.wait()

    for copy in lab_copies:
        copy.wait()
    for g in range(2):
        part_copies[g].wait()
        here = pl.ds(g * slots, slots)
        home[here, :] = (part[here, :].astype(F32) + part_in[here, :].astype(F32)).astype(BF16)
    half_c = pl.ds(pl.multiple_of(c * half, half), half)
    half_o = pl.ds(pl.multiple_of((1 - c) * half, half), half)

    def ext1(which_half):
        return sl.at[which_half]

    ext1_copy = remote(home.at[half_c], ext1(half_c), 2, m_dev(-1))
    ext1_copy.start()
    ext2_copy = remote(home.at[pl.ds(slots, slots)], sl.at[pl.ds(slots, slots)], 3, m_dev(1 - 2 * c))

    @pl.when(c == 0)
    def _():
        ext2_copy.start()

    text_copy.wait()

    factor = scale_ref[...]
    factor2 = factor * LOG2E
    offset2 = bias_ref[...] * LOG2E
    sums_ref[...] = jnp.zeros_like(sums_ref)

    def add(x, y):
        return x + y

    def scores(o, n, slot_rows):
        wide = n * slots
        inner_ref[:, :wide] = mm_nt(text_ref[...], slot_rows)
        labels = lab[o] if n == 1 else jnp.concatenate([lab[o], lab[o + 1]], axis=1)

        def chunk(j, sums):
            at = pl.multiple_of(j * t_tile, t_tile)
            inner = inner_ref[pl.ds(at, t_tile), :wide]
            logits = factor2 * inner + offset2
            e = jnp.exp2(-jnp.abs(logits))
            u = 1.0 + e
            r = pl.reciprocal(u, approx=True)
            r = r * (2.0 - u * r)
            sig = jnp.where(logits >= 0.0, r, e * r)
            positive = iota((t_tile, wide), 0) == labels - (d * texts + at)
            grad = jnp.where(positive, sig - 1.0, sig)
            linear = jnp.maximum(jnp.where(positive, -logits, logits), 0.0)
            wt[pl.ds(at, t_tile), o * slots : o * slots + wide] = grad.astype(BF16)
            log_u = jnp.log(fold(u, lambda x, y: x * y))
            return (
                sums[0] + fold(linear, add),
                sums[1] + log_u + fold(e - (u - 1.0), add),
                sums[2] + fold(grad * inner, add),
                sums[3] + fold(grad, add),
            )

        sums = lax.fori_loop(0, texts // t_tile, chunk, (jnp.zeros((8, wide), F32),) * 4)
        for k in range(4):
            for g in range(n):
                sums_ref[k] += sums[k][:, g * slots : (g + 1) * slots]

    def image_terms(o, n):
        return mm_tn(wt[:, o * slots : (o + n) * slots], text_ref[...])

    n_text = text_half // t_tile
    mine = pl.ds(pl.multiple_of(s * text_half, text_half), text_half)
    theirs = pl.ds(pl.multiple_of((1 - s) * text_half, text_half), text_half)

    scores(0, 2, home[...])

    own[...] = image_terms(0, 2)
    own_copy = remote(own, own_in, 4, partner)
    own_copy.start()

    @pl.when(c == 1)
    def _():
        ext2_copy.start()

    text_sum[...] = mm(wt[theirs, : 2 * slots], home[...])

    ext1_copy.wait_recv()
    ext1_fwd = remote(ext1(half_c), ext1(half_c), 5, partner)
    ext1_fwd.start()
    pre_copy = remote(pre.at[half_o], pre_in, 6, partner)
    ret1_copy = remote(ret1_out, ret1.at[half_c], 8, m_dev(1))
    ret2_copy = remote(ret2_out, ret2, 7, m_dev(2 * c - 1))
    text_copies = []
    for j in range(n_text):
        here = pl.ds(j * t_tile, t_tile)
        text_copies.append(remote(text_out.at[here], text_in.at[here], 15 + j, across))

    def send_text(o):
        for j in range(n_text):
            here = pl.ds(j * t_tile, t_tile)
            at = pl.ds(pl.multiple_of((1 - s) * text_half + j * t_tile, t_tile), t_tile)
            late = mm(wt[at, o * slots :], sl[(o - 2) * slots :, :])
            text_out[here, :] = (text_sum[here, :] + late).astype(BF16)
            text_copies[j].start()

    def send_pre():
        pre[...] = image_terms(2, 1)
        pre_copy.start()

    def send_ret1():
        pre_copy.wait_recv()
        ret1_out[...] = (pre[half_c, :] + pre_in[...]).astype(BF16)
        ret1_copy.start()

    def send_ret2():
        ret2_out[...] = image_terms(3, 1).astype(BF16)
        ret2_copy.start()

    @pl.when(c == 0)
    def _():
        ext2_copy.wait_recv()
        scores(3, 1, sl[slots:, :])
        ext1_fwd.wait_recv()
        scores(2, 1, sl[:slots, :])
        send_text(2)
        send_pre()
        send_ret1()
        send_ret2()

    @pl.when(c == 1)
    def _():
        ext1_fwd.wait_recv()
        scores(2, 1, sl[:slots, :])
        send_pre()
        text_sum[...] += mm(wt[theirs, 2 * slots : 3 * slots], sl[:slots, :])
        ext2_copy.wait_recv()
        scores(3, 1, sl[slots:, :])
        send_ret1()
        send_ret2()
        send_text(3)

    lane = iota((1, LANES), 1)
    totals = [
        jnp.sum(x, keepdims=True)
        for x in (LN2 * sums_ref[0] + sums_ref[1], sums_ref[2], sums_ref[3])
    ]
    stat[...] = jnp.where(lane == 0, totals[0], jnp.where(lane == 1, totals[1], totals[2]))
    stat_copy = remote(stat, stat_in, 9, partner)
    stat_copy.start()
    gt[...] = mm(wt[mine, : 2 * slots], home[...]) + mm(wt[mine, 2 * slots :], sl[...])
    gt_copy = pltpu.make_async_copy(gt, gt_hbm, local_sem.at[5])
    gt_copy.start()
    stat_copy.wait()
    stat[...] = stat[...] + stat_in[...]
    own_stats, all_stats = all_start(
        lambda k: stat, lambda k: stats_in.at[chip], stat, stats_in.at[chip], stats_in, 2, 1
    )

    ret1_copy.wait_recv()
    ret1_fwd = remote(ret1.at[half_c], ret1.at[half_c], 13, partner)
    ret1_fwd.start()
    own_copy.wait_recv()
    ret1_fwd.wait_recv()
    total = own[:slots, :] + own_in[:slots, :] + ret1[...].astype(F32)
    grad_rows[:slots, :] = (factor * total).astype(BF16)
    ret2_copy.wait_recv()
    ret2_fwd = remote(ret2, ret2b, 14, partner)
    ret2_fwd.start()
    ret2_fwd.wait_recv()
    total = own[slots:, :] + own_in[slots:, :] + (ret2[...].astype(F32) + ret2b[...].astype(F32))
    grad_rows[slots:, :] = (factor * total).astype(BF16)

    parts = 4 if chips >= 32 else 1
    n = chips // parts
    for r in range(parts):
        out = mm(q_t[r * rows // parts : (r + 1) * rows // parts, :], grad_rows[...])
        tiles = [
            out[:, b : b + LANES].reshape(n, per_chip, LANES) for b in range(0, columns, LANES)
        ]
        back[r * n : (r + 1) * n] = jnp.concatenate(tiles, axis=1).astype(BF16)
    own_back, all_back = all_start(
        lambda k: back.at[k], lambda k: back_in.at[k], back.at[last], back_in.at[last], back_in, 1, -1
    )

    for copy in text_copies:
        copy.wait_recv()
    placed_copy.wait()
    gt_copy.wait()
    own_stats.wait()
    all_stats.wait()
    own_back.wait()
    all_back.wait()
    out_all.wait_send()
    for copy in (
        ext1_copy,
        ext2_copy,
        own_copy,
        ext1_fwd,
        pre_copy,
        ret2_copy,
        ret1_copy,
        ret1_fwd,
        ret2_fwd,
        *text_copies,
    ):
        copy.wait_send()


def finish(n_dp, pairs, per_chip, scale_ref, back_ref, stats_ref, text_in_ref, gt_in_ref, *rest):
    placed_ref, gi_ref, gt_ref, loss_ref, gscale_ref, gbias_ref, rows_in, placed_col = rest
    tile, columns = gi_ref.shape
    pack = rows_in.shape[0]
    step = pl.program_id(0)

    @pl.when(step == 0)
    def _():
        for b in range(columns // LANES):
            block = back_ref[:, b * per_chip : (b + 1) * per_chip, :].astype(F32)
            rows_in[:, b * LANES : (b + 1) * LANES] = block.reshape(pack, LANES).astype(BF16)
        placed = jnp.broadcast_to(placed_ref[...].astype(F32), (LANES, placed_col.shape[0]))
        placed_col[...] = jnp.transpose(placed).astype(jnp.int32)
        total = jnp.sum(stats_ref[...], axis=0)
        lane = iota((1, LANES), 1)
        for k, ref in enumerate((loss_ref, gscale_ref, gbias_ref)):
            ref[0] = jnp.sum(jnp.where(lane == k, total, 0.0)) / pairs

    placed = placed_col[pl.ds(pl.multiple_of(step * tile, tile), tile), :1]
    choose = (placed == iota((tile, pack), 1)).astype(F32).astype(BF16)
    gi_ref[...] = mm(choose, rows_in[...]).astype(BF16)
    gt_ref[...] = scale_ref[...] * (gt_in_ref[...] + text_in_ref[...].astype(F32))


def local(images, text_embeds, dest_slot, labels, logit_scale, logit_bias):
    n_dp = lax.axis_size("dp")
    rows, columns = images.shape
    texts = text_embeds.shape[0]
    slots = labels.shape[0]
    chips = n_dp
    per_chip = rows // chips
    width = (columns + LANES) // 2
    pairs = float(slots * n_dp * 2 * STOPS * texts)
    vmem = pl.BlockSpec(memory_space=pltpu.VMEM)
    smem = pl.BlockSpec(memory_space=pltpu.SMEM)
    hbm = pl.BlockSpec(memory_space=pl.ANY)
    message = pltpu.VMEM((chips, 2 * per_chip, width), BF16)
    tiled = (chips, per_chip * columns // LANES, LANES)

    def buf(n, dtype=BF16):
        return pltpu.VMEM((n, columns), dtype)

    scale = logit_scale.reshape(1, 1)
    back, stats, text_in, gt, placed = pl.pallas_call(
        functools.partial(kernel, n_dp),
        out_shape=(
            jax.ShapeDtypeStruct(tiled, BF16),
            jax.ShapeDtypeStruct((chips, 1, LANES), F32),
            jax.ShapeDtypeStruct((texts // 2, columns), BF16),
            jax.ShapeDtypeStruct((texts // 2, columns), F32),
            jax.ShapeDtypeStruct((1, rows), jnp.int32),
        ),
        in_specs=[vmem, vmem, vmem, vmem, vmem, hbm],
        out_specs=(hbm, hbm, hbm, hbm, hbm),
        scratch_shapes=[
            buf(texts),
            message,
            message,
            pltpu.VMEM(tiled, BF16),
            buf(2 * slots),
            buf(2 * slots),
            buf(2 * slots),
            buf(2 * slots),
            pltpu.VMEM((4, 1, slots), jnp.int32),
            pltpu.VMEM((texts, 4 * slots), BF16),
            pltpu.VMEM((texts, 2 * slots), F32),
            pltpu.VMEM((4, 8, slots), F32),
            buf(2 * slots, F32),
            buf(2 * slots, F32),
            buf(slots, F32),
            buf(slots // 2, F32),
            buf(slots // 2),
            buf(slots),
            buf(slots),
            buf(slots),
            buf(slots),
            buf(2 * slots),
            buf(texts // 2, F32),
            buf(texts // 2),
            buf(texts // 2, F32),
            pltpu.VMEM((1, rows), jnp.int32),
            pltpu.VMEM((rows, 2 * slots), BF16),
            pltpu.VMEM((1, LANES), F32),
            pltpu.VMEM((1, LANES), F32),
            pltpu.SemaphoreType.DMA((3,)),
            pltpu.SemaphoreType.DMA((3,)),
            pltpu.SemaphoreType.DMA((8,)),
            pltpu.SemaphoreType.DMA((24,)),
            pltpu.SemaphoreType.DMA((24,)),
        ],
        compiler_params=pltpu.CompilerParams(
            collective_id=0,
            has_side_effects=True,
            vmem_limit_bytes=58 * 1024 * 1024,
        ),
    )(
        scale,
        logit_bias.reshape(1, 1),
        dest_slot.reshape(1, rows),
        labels.reshape(1, slots),
        images,
        text_embeds,
    )
    tiles = 2
    tile_rows = pl.BlockSpec((rows // tiles, columns), lambda i: (i, 0))
    tile_texts = pl.BlockSpec((texts // 2 // tiles, columns), lambda i: (i, 0))
    scalar = jax.ShapeDtypeStruct((1,), F32)
    return pl.pallas_call(
        functools.partial(finish, n_dp, pairs, per_chip),
        out_shape=(
            jax.ShapeDtypeStruct((rows, columns), BF16),
            jax.ShapeDtypeStruct((texts // 2, columns), F32),
            scalar,
            scalar,
            scalar,
        ),
        grid=(tiles,),
        in_specs=[
            pl.BlockSpec((1, 1), lambda i: (0, 0)),
            pl.BlockSpec(back.shape, lambda i: (0, 0, 0)),
            pl.BlockSpec(stats.shape, lambda i: (0, 0, 0)),
            tile_texts,
            tile_texts,
            pl.BlockSpec((1, rows), lambda i: (0, 0)),
        ],
        out_specs=(tile_rows, tile_texts, smem, smem, smem),
        scratch_shapes=[buf(rows), pltpu.VMEM((rows, LANES), jnp.int32)],
        compiler_params=pltpu.CompilerParams(vmem_limit_bytes=60 * 1024 * 1024),
    )(scale, back, stats, text_in, gt, placed)


def solution(mesh):
    return jax.shard_map(
        local,
        mesh=mesh,
        in_specs=(
            P(("dp", "sub"), None),
            P("dp", None),
            P(("dp", "sub")),
            P(("dp", "sub")),
            P(),
            P(),
        ),
        out_specs=(P(("dp", "sub"), None), P(("dp", "sub"), None), P(), P(), P()),
        check_vma=False,
    )
```

```python
import functools

import jax
import jax.numpy as jnp
from jax import lax
from jax.experimental import pallas as pl
from jax.experimental.pallas import tpu as pltpu
from jax.sharding import PartitionSpec as P

STOPS = 4
LANES = 128
MESH = pl.DeviceIdType.MESH
STRIDE, UNSTRIDE = 27, 19
LOG2E = 1.4426950408889634
LN2 = 0.6931471805599453
F32 = jnp.float32
BF16 = jnp.bfloat16


def iota(shape, axis):
    return lax.broadcasted_iota(jnp.int32, shape, axis)


def mm(a, b):
    return lax.dot_general(a, b, (((1,), (0,)), ((), ())), preferred_element_type=F32)


def mm_tn(a, b):
    return lax.dot_general(a, b, (((0,), (0,)), ((), ())), preferred_element_type=F32)


def fold(x, op):
    while x.shape[0] > 8:
        n = x.shape[0] // 2
        x = op(x[:n], x[n:])
    return x


def mm_nt(a, b):
    return lax.dot_general(a, b, (((1,), (1,)), ((), ())), preferred_element_type=F32)


def kernel(
    n_dp,
    scale_ref,
    bias_ref,
    dest_ref,
    labels_ref,
    images_ref,
    text_hbm,
    back_in,
    stats_in,
    text_in,
    gt_hbm,
    placed_hbm,
    text_ref,
    send,
    recv,
    back,
    home,
    part,
    part_in,
    sl,
    lab,
    wt,
    inner_ref,
    sums_ref,
    own,
    own_in,
    pre,
    pre_in,
    ret1_out,
    ret1,
    ret2_out,
    ret2,
    ret2b,
    grad_rows,
    text_sum,
    text_out,
    gt,
    placed_ref,
    q_t,
    stat,
    stat_in,
    a2a_send,
    a2a_recv,
    local_sem,
    ss,
    rs,
):
    rows, columns = images_ref.shape
    texts = text_ref.shape[0]
    text_half = texts // 2
    slots = labels_ref.shape[1]
    half = slots // 2
    chips = n_dp
    n_m = n_dp // 2
    per_chip = rows // chips
    width = send.shape[2]
    tail = columns - width
    t_tile = min(256, texts // 2)

    d = lax.axis_index("dp")
    s = lax.axis_index("sub")
    m = lax.div(d, 2)
    c = lax.rem(d, 2)
    chip = m * 2 + s
    upper = lax.div(m, n_m // 2)
    half_here = lax.rem(s + upper, 2)
    partner = (m * 2 + (1 - c), s)
    across = (d, 1 - s)

    def chip_dev(i):
        i = lax.rem(i + chips, chips)
        return (lax.div(i, 2) * 2 + c, lax.rem(i, 2))

    def m_dev(step):
        there = lax.rem(m + step + n_m, n_m)
        return (there * 2 + c, lax.rem(half_here + lax.div(there, n_m // 2), 2))

    def labels_to(step):
        there = lax.rem(d - step + n_dp, n_dp)
        return (there, lax.rem(s + lax.div(there, n_dp // 2), 2))

    def labels_from(step):
        return (lax.rem(d + step, n_dp), half_here)

    text_copy = pltpu.make_async_copy(text_hbm, text_ref, local_sem.at[7])
    text_copy.start()

    barrier = pltpu.get_barrier_semaphore()

    def greet(k, carry):
        pl.semaphore_signal(barrier, inc=1, device_id=chip_dev(chip + k), device_id_type=MESH)
        return carry

    lax.fori_loop(1, chips, greet, 0)
    for dev in (partner, labels_from(1), labels_from(3)):
        pl.semaphore_signal(barrier, inc=1, device_id=dev, device_id_type=MESH)

    def remote(src, dst, k, dev):
        return pltpu.make_async_remote_copy(
            src_ref=src,
            dst_ref=dst,
            send_sem=ss.at[k],
            recv_sem=rs.at[k],
            device_id=dev,
            device_id_type=MESH,
        )

    q = dest_ref[...]
    valid = q >= 0
    group = lax.div(jnp.maximum(q, 0), 2 * slots)
    rest = jnp.maximum(q, 0) - group * (2 * slots)
    to_sub = lax.div(rest, slots)
    slot_id = rest - to_sub * slots
    even = (group & 1) == 0
    to_m = lax.div((group + (n_dp - 1)) & (n_dp - 1), 2)
    to_sub = (to_sub + lax.div(to_m, n_m // 2)) & 1
    rel = ((to_m * 2 + to_sub - chip + chips) * UNSTRIDE + (chips - 1)) & (chips - 1)
    rel = jnp.where(valid, rel, -1)
    onehot = rel == iota((chips, rows), 0)
    earlier = (iota((rows, rows), 0) < iota((rows, rows), 1)).astype(F32).astype(BF16)
    onehot_f = onehot.astype(F32)
    rank = mm(onehot_f.astype(BF16), earlier)
    within = jnp.sum(onehot_f * rank, axis=0, keepdims=True)
    placed = jnp.where(valid, rel.astype(F32) * float(per_chip) + within, -1.0)
    placed_int = placed.astype(jnp.int32)
    placed_ref[...] = placed_int
    placed_copy = pltpu.make_async_copy(placed_ref, placed_hbm, local_sem.at[4])
    placed_copy.start()
    id_plus = (slot_id + 1).astype(F32)
    id_odd = jnp.where(valid & jnp.logical_not(even), id_plus, 0.0)
    id_even = jnp.where(valid & even, id_plus, 0.0)
    which = iota((LANES, rows), 0)
    id_rows = jnp.where(which == 0, id_odd, jnp.where(which == 1, id_even, 0.0))
    ids_block = jnp.transpose(id_rows).astype(BF16)
    row_tile = min(128, rows)
    for r in range(rows // row_tile):
        p_mat = (placed_int == iota((row_tile, rows), 0) + r * row_tile).astype(F32).astype(BF16)
        n = row_tile // per_chip
        first = mm(p_mat, images_ref[:, :width]).reshape(n, per_chip, width)
        second = mm(p_mat, images_ref[:, width:]).reshape(n, per_chip, tail)
        third = mm(p_mat, ids_block).reshape(n, per_chip, LANES)
        second = jnp.concatenate([second, third], axis=2)
        send[r * n : (r + 1) * n] = jnp.concatenate([first, second], axis=1).astype(BF16)

    pl.semaphore_wait(barrier, chips - 1 + 3)

    lab_copies = [
        remote(labels_ref, lab.at[slot], 9 + step, labels_to(step))
        for step, slot in ((1, 1 - c), (2, 1 + c), (3, 3 - c))
    ]
    for copy in lab_copies:
        copy.start()
    lab_own = pltpu.make_async_copy(labels_ref, lab.at[3 - 3 * c], local_sem.at[6])
    lab_swap = remote(labels_ref, lab.at[3 - 3 * c], 20, across)

    @pl.when(upper == 0)
    def _():
        lab_own.start()

    @pl.when(upper == 1)
    def _():
        lab_swap.start()


    def all_start(src, dst, own_src, own_dst, total, which_sem, sign):
        def step(k, carry):
            to = lax.rem(chip + sign * lax.rem((k + 1) * STRIDE, chips) + chips, chips)
            swaps = lax.rem(to, 2) + s + lax.div(to, chips // 2) + upper

            @pl.when(lax.rem(swaps, 2) == carry)
            def _():
                pltpu.make_async_remote_copy(
                    src_ref=src(k),
                    dst_ref=dst(k),
                    send_sem=a2a_send.at[which_sem],
                    recv_sem=a2a_recv.at[which_sem],
                    device_id=chip_dev(to),
                    device_id_type=MESH,
                ).start()

            return carry

        def step_any(k, carry):
            pltpu.make_async_remote_copy(
                src_ref=src(k),
                dst_ref=dst(k),
                send_sem=a2a_send.at[which_sem],
                recv_sem=a2a_recv.at[which_sem],
                device_id=chip_dev(chip + sign * lax.rem((k + 1) * STRIDE, chips)),
                device_id_type=MESH,
            ).start()
            return carry

        if which_sem == 0:
            lax.fori_loop(0, chips - 1, step_any, 0)
        else:
            for turn in (1, 0):
                lax.fori_loop(0, chips - 1, step, turn)
        own_copy = pltpu.make_async_copy(own_src, own_dst, local_sem.at[which_sem])
        own_copy.start()
        all_copy = pltpu.make_async_remote_copy(
            src_ref=total.at[pl.ds(0, chips - 1)],
            dst_ref=total.at[pl.ds(0, chips - 1)],
            send_sem=a2a_send.at[which_sem],
            recv_sem=a2a_recv.at[which_sem],
            device_id=partner,
            device_id_type=MESH,
        )
        return own_copy, all_copy

    last = chips - 1
    out_own, out_all = all_start(
        lambda k: send.at[k], lambda k: recv.at[k], send.at[last], recv.at[last], recv, 0, 1
    )
    out_own.wait()
    out_all.wait_recv()

    ids = recv[:, per_chip:, tail:].astype(F32).reshape(rows, LANES).astype(jnp.int32)
    lane = iota((rows, 2 * slots), 1)
    filled = jnp.where(lane < slots, ids[:, :1], ids[:, 1:2] + slots)
    q_t[...] = (filled == lane + 1).astype(F32).astype(BF16)
    ids_t = jnp.transpose(ids.astype(F32)).astype(jnp.int32)
    first = recv[:, :per_chip, :].astype(F32).reshape(rows, width).astype(BF16)
    second = recv[:, per_chip:, :tail].astype(F32).reshape(rows, tail).astype(BF16)
    part_copies = []
    for g in range(2):
        q_mat = (ids_t[g : g + 1, :] == iota((slots, rows), 0) + 1).astype(F32).astype(BF16)
        here = pl.ds(g * slots, slots)
        part[here, :width] = mm(q_mat, first).astype(BF16)
        part[here, width:] = mm(q_mat, second).astype(BF16)
        copy = remote(part.at[here], part_in.at[here], g, partner)
        copy.start()
        part_copies.append(copy)

    @pl.when(upper == 0)
    def _():
        lab_own.wait()

    @pl.when(upper == 1)
    def _():
        lab_swap.wait()

    for copy in lab_copies:
        copy.wait()
    for g in range(2):
        part_copies[g].wait()
        here = pl.ds(g * slots, slots)
        home[here, :] = (part[here, :].astype(F32) + part_in[here, :].astype(F32)).astype(BF16)
    half_c = pl.ds(pl.multiple_of(c * half, half), half)
    half_o = pl.ds(pl.multiple_of((1 - c) * half, half), half)

    def ext1(which_half):
        return sl.at[which_half]

    ext1_copy = remote(home.at[half_c], ext1(half_c), 2, m_dev(-1))
    ext1_copy.start()
    ext2_copy = remote(home.at[pl.ds(slots, slots)], sl.at[pl.ds(slots, slots)], 3, m_dev(1 - 2 * c))

    @pl.when(c == 0)
    def _():
        ext2_copy.start()

    text_copy.wait()

    factor = scale_ref[...]
    factor2 = factor * LOG2E
    offset2 = bias_ref[...] * LOG2E
    sums_ref[...] = jnp.zeros_like(sums_ref)

    def add(x, y):
        return x + y

    def scores(o, n, slot_rows):
        wide = n * slots
        inner_ref[:, :wide] = mm_nt(text_ref[...], slot_rows)
        labels = lab[o] if n == 1 else jnp.concatenate([lab[o], lab[o + 1]], axis=1)

        def chunk(j, sums):
            at = pl.multiple_of(j * t_tile, t_tile)
            inner = inner_ref[pl.ds(at, t_tile), :wide]
            logits = factor2 * inner + offset2
            e = jnp.exp2(-jnp.abs(logits))
            u = 1.0 + e
            r = pl.reciprocal(u, approx=True)
            r = r * (2.0 - u * r)
            sig = jnp.where(logits >= 0.0, r, e * r)
            positive = iota((t_tile, wide), 0) == labels - (d * texts + at)
            grad = jnp.where(positive, sig - 1.0, sig)
            linear = jnp.maximum(jnp.where(positive, -logits, logits), 0.0)
            wt[pl.ds(at, t_tile), o * slots : o * slots + wide] = grad.astype(BF16)
            log_u = jnp.log(fold(u, lambda x, y: x * y))
            return (
                sums[0] + fold(linear, add),
                sums[1] + log_u + fold(e - (u - 1.0), add),
                sums[2] + fold(grad * inner, add),
                sums[3] + fold(grad, add),
            )

        sums = lax.fori_loop(0, texts // t_tile, chunk, (jnp.zeros((8, wide), F32),) * 4)
        for k in range(4):
            for g in range(n):
                sums_ref[k] += sums[k][:, g * slots : (g + 1) * slots]

    def image_terms(o, n):
        return mm_tn(wt[:, o * slots : (o + n) * slots], text_ref[...])

    n_text = text_half // t_tile
    mine = pl.ds(pl.multiple_of(s * text_half, text_half), text_half)
    theirs = pl.ds(pl.multiple_of((1 - s) * text_half, text_half), text_half)

    scores(0, 2, home[...])

    own[...] = image_terms(0, 2)
    own_copy = remote(own, own_in, 4, partner)
    own_copy.start()

    @pl.when(c == 1)
    def _():
        ext2_copy.start()

    text_sum[...] = mm(wt[theirs, : 2 * slots], home[...])

    ext1_copy.wait_recv()
    ext1_fwd = remote(ext1(half_c), ext1(half_c), 5, partner)
    ext1_fwd.start()
    pre_copy = remote(pre.at[half_o], pre_in, 6, partner)
    ret1_copy = remote(ret1_out, ret1.at[half_c], 8, m_dev(1))
    ret2_copy = remote(ret2_out, ret2, 7, m_dev(2 * c - 1))
    text_copies = []
    for j in range(n_text):
        here = pl.ds(j * t_tile, t_tile)
        text_copies.append(remote(text_out.at[here], text_in.at[here], 15 + j, across))

    def send_text(o):
        for j in range(n_text):
            here = pl.ds(j * t_tile, t_tile)
            at = pl.ds(pl.multiple_of((1 - s) * text_half + j * t_tile, t_tile), t_tile)
            late = mm(wt[at, o * slots :], sl[(o - 2) * slots :, :])
            text_out[here, :] = (text_sum[here, :] + late).astype(BF16)
            text_copies[j].start()

    def send_pre():
        pre[...] = image_terms(2, 1)
        pre_copy.start()

    def send_ret1():
        pre_copy.wait_recv()
        ret1_out[...] = (pre[half_c, :] + pre_in[...]).astype(BF16)
        ret1_copy.start()

    def send_ret2():
        ret2_out[...] = image_terms(3, 1).astype(BF16)
        ret2_copy.start()

    @pl.when(c == 0)
    def _():
        ext2_copy.wait_recv()
        scores(3, 1, sl[slots:, :])
        ext1_fwd.wait_recv()
        scores(2, 1, sl[:slots, :])
        send_text(2)
        send_pre()
        send_ret1()
        send_ret2()

    @pl.when(c == 1)
    def _():
        ext1_fwd.wait_recv()
        scores(2, 1, sl[:slots, :])
        send_pre()
        text_sum[...] += mm(wt[theirs, 2 * slots : 3 * slots], sl[:slots, :])
        send_ret1()
        ext2_copy.wait_recv()
        scores(3, 1, sl[slots:, :])
        send_text(3)
        send_ret2()

    lane = iota((1, LANES), 1)
    totals = [
        jnp.sum(x, keepdims=True)
        for x in (LN2 * sums_ref[0] + sums_ref[1], sums_ref[2], sums_ref[3])
    ]
    stat[...] = jnp.where(lane == 0, totals[0], jnp.where(lane == 1, totals[1], totals[2]))
    stat_copy = remote(stat, stat_in, 9, partner)
    stat_copy.start()
    gt[...] = mm(wt[mine, : 2 * slots], home[...]) + mm(wt[mine, 2 * slots :], sl[...])
    gt_copy = pltpu.make_async_copy(gt, gt_hbm, local_sem.at[5])
    gt_copy.start()
    stat_copy.wait()
    stat[...] = stat[...] + stat_in[...]
    own_stats, all_stats = all_start(
        lambda k: stat, lambda k: stats_in.at[chip], stat, stats_in.at[chip], stats_in, 2, 1
    )

    ret1_copy.wait_recv()
    ret1_fwd = remote(ret1.at[half_c], ret1.at[half_c], 13, partner)
    ret1_fwd.start()
    own_copy.wait_recv()
    ret1_fwd.wait_recv()
    total = own[:slots, :] + own_in[:slots, :] + ret1[...].astype(F32)
    grad_rows[:slots, :] = (factor * total).astype(BF16)
    ret2_copy.wait_recv()
    ret2_fwd = remote(ret2, ret2b, 14, partner)
    ret2_fwd.start()
    ret2_fwd.wait_recv()
    total = own[slots:, :] + own_in[slots:, :] + (ret2[...].astype(F32) + ret2b[...].astype(F32))
    grad_rows[slots:, :] = (factor * total).astype(BF16)

    parts = 4 if chips >= 32 else 1
    n = chips // parts
    for r in range(parts):
        out = mm(q_t[r * rows // parts : (r + 1) * rows // parts, :], grad_rows[...])
        tiles = [
            out[:, b : b + LANES].reshape(n, per_chip, LANES) for b in range(0, columns, LANES)
        ]
        back[r * n : (r + 1) * n] = jnp.concatenate(tiles, axis=1).astype(BF16)
    own_back, all_back = all_start(
        lambda k: back.at[k], lambda k: back_in.at[k], back.at[last], back_in.at[last], back_in, 1, -1
    )

    for copy in text_copies:
        copy.wait_recv()
    placed_copy.wait()
    gt_copy.wait()
    own_stats.wait()
    all_stats.wait()
    own_back.wait()
    all_back.wait()
    out_all.wait_send()
    for copy in (
        ext1_copy,
        ext2_copy,
        own_copy,
        ext1_fwd,
        pre_copy,
        ret2_copy,
        ret1_copy,
        ret1_fwd,
        ret2_fwd,
        *text_copies,
    ):
        copy.wait_send()


def finish(n_dp, pairs, per_chip, scale_ref, back_ref, stats_ref, text_in_ref, gt_in_ref, *rest):
    placed_ref, gi_ref, gt_ref, loss_ref, gscale_ref, gbias_ref, rows_in, placed_col = rest
    tile, columns = gi_ref.shape
    pack = rows_in.shape[0]
    step = pl.program_id(0)

    @pl.when(step == 0)
    def _():
        for b in range(columns // LANES):
            block = back_ref[:, b * per_chip : (b + 1) * per_chip, :].astype(F32)
            rows_in[:, b * LANES : (b + 1) * LANES] = block.reshape(pack, LANES).astype(BF16)
        placed = jnp.broadcast_to(placed_ref[...].astype(F32), (LANES, placed_col.shape[0]))
        placed_col[...] = jnp.transpose(placed).astype(jnp.int32)
        total = jnp.sum(stats_ref[...], axis=0)
        lane = iota((1, LANES), 1)
        for k, ref in enumerate((loss_ref, gscale_ref, gbias_ref)):
            ref[0] = jnp.sum(jnp.where(lane == k, total, 0.0)) / pairs

    placed = placed_col[pl.ds(pl.multiple_of(step * tile, tile), tile), :1]
    choose = (placed == iota((tile, pack), 1)).astype(F32).astype(BF16)
    gi_ref[...] = mm(choose, rows_in[...]).astype(BF16)
    gt_ref[...] = scale_ref[...] * (gt_in_ref[...] + text_in_ref[...].astype(F32))


def local(images, text_embeds, dest_slot, labels, logit_scale, logit_bias):
    n_dp = lax.axis_size("dp")
    rows, columns = images.shape
    texts = text_embeds.shape[0]
    slots = labels.shape[0]
    chips = n_dp
    per_chip = rows // chips
    width = (columns + LANES) // 2
    pairs = float(slots * n_dp * 2 * STOPS * texts)
    vmem = pl.BlockSpec(memory_space=pltpu.VMEM)
    smem = pl.BlockSpec(memory_space=pltpu.SMEM)
    hbm = pl.BlockSpec(memory_space=pl.ANY)
    message = pltpu.VMEM((chips, 2 * per_chip, width), BF16)
    tiled = (chips, per_chip * columns // LANES, LANES)

    def buf(n, dtype=BF16):
        return pltpu.VMEM((n, columns), dtype)

    scale = logit_scale.reshape(1, 1)
    back, stats, text_in, gt, placed = pl.pallas_call(
        functools.partial(kernel, n_dp),
        out_shape=(
            jax.ShapeDtypeStruct(tiled, BF16),
            jax.ShapeDtypeStruct((chips, 1, LANES), F32),
            jax.ShapeDtypeStruct((texts // 2, columns), BF16),
            jax.ShapeDtypeStruct((texts // 2, columns), F32),
            jax.ShapeDtypeStruct((1, rows), jnp.int32),
        ),
        in_specs=[vmem, vmem, vmem, vmem, vmem, hbm],
        out_specs=(hbm, hbm, hbm, hbm, hbm),
        scratch_shapes=[
            buf(texts),
            message,
            message,
            pltpu.VMEM(tiled, BF16),
            buf(2 * slots),
            buf(2 * slots),
            buf(2 * slots),
            buf(2 * slots),
            pltpu.VMEM((4, 1, slots), jnp.int32),
            pltpu.VMEM((texts, 4 * slots), BF16),
            pltpu.VMEM((texts, 2 * slots), F32),
            pltpu.VMEM((4, 8, slots), F32),
            buf(2 * slots, F32),
            buf(2 * slots, F32),
            buf(slots, F32),
            buf(slots // 2, F32),
            buf(slots // 2),
            buf(slots),
            buf(slots),
            buf(slots),
            buf(slots),
            buf(2 * slots),
            buf(texts // 2, F32),
            buf(texts // 2),
            buf(texts // 2, F32),
            pltpu.VMEM((1, rows), jnp.int32),
            pltpu.VMEM((rows, 2 * slots), BF16),
            pltpu.VMEM((1, LANES), F32),
            pltpu.VMEM((1, LANES), F32),
            pltpu.SemaphoreType.DMA((3,)),
            pltpu.SemaphoreType.DMA((3,)),
            pltpu.SemaphoreType.DMA((8,)),
            pltpu.SemaphoreType.DMA((24,)),
            pltpu.SemaphoreType.DMA((24,)),
        ],
        compiler_params=pltpu.CompilerParams(
            collective_id=0,
            has_side_effects=True,
            vmem_limit_bytes=58 * 1024 * 1024,
        ),
    )(
        scale,
        logit_bias.reshape(1, 1),
        dest_slot.reshape(1, rows),
        labels.reshape(1, slots),
        images,
        text_embeds,
    )
    tiles = 2
    tile_rows = pl.BlockSpec((rows // tiles, columns), lambda i: (i, 0))
    tile_texts = pl.BlockSpec((texts // 2 // tiles, columns), lambda i: (i, 0))
    scalar = jax.ShapeDtypeStruct((1,), F32)
    return pl.pallas_call(
        functools.partial(finish, n_dp, pairs, per_chip),
        out_shape=(
            jax.ShapeDtypeStruct((rows, columns), BF16),
            jax.ShapeDtypeStruct((texts // 2, columns), F32),
            scalar,
            scalar,
            scalar,
        ),
        grid=(tiles,),
        in_specs=[
            pl.BlockSpec((1, 1), lambda i: (0, 0)),
            pl.BlockSpec(back.shape, lambda i: (0, 0, 0)),
            pl.BlockSpec(stats.shape, lambda i: (0, 0, 0)),
            tile_texts,
            tile_texts,
            pl.BlockSpec((1, rows), lambda i: (0, 0)),
        ],
        out_specs=(tile_rows, tile_texts, smem, smem, smem),
        scratch_shapes=[buf(rows), pltpu.VMEM((rows, LANES), jnp.int32)],
        compiler_params=pltpu.CompilerParams(vmem_limit_bytes=60 * 1024 * 1024),
    )(scale, back, stats, text_in, gt, placed)


def solution(mesh):
    return jax.shard_map(
        local,
        mesh=mesh,
        in_specs=(
            P(("dp", "sub"), None),
            P("dp", None),
            P(("dp", "sub")),
            P(("dp", "sub")),
            P(),
            P(),
        ),
        out_specs=(P(("dp", "sub"), None), P(("dp", "sub"), None), P(), P(), P()),
        check_vma=False,
    )
```
